32 devices in a mesh: nodes: 16 (over z, y, core), feat: 2 (over x).
Axes of the slice: x: 2, y: 2, z: 4, core: 2. Of those that a mesh axis runs over, the one named last changes fastest.
Arguments:
- node_feats: float32 [4096, 768], P(('nodes', 'feat')), may hold values from -6 to 6
- rel_weights: float32 [5, 512, 768], P(None, 'feat'), may hold values from -0.21875 to 0.21875
- self_weight: float32 [512, 768], P('feat'), may hold values from -0.21875 to 0.21875
- cotangent: float32 [512, 4096], P('feat', 'nodes'), may hold values from -6 to 6
- tile_values: bfloat16 [16, 5, 6, 128, 128], P('nodes'), may hold values from 0 to 0.049804688
- tile_peer: int32 [16, 5, 6], P('nodes'), may hold values from 0 to 15, as said below
- tile_slot: int32 [16, 5, 6], P('nodes'), may hold values from 0 to 1, as said below
- tile_target: int32 [16, 5, 6], P('nodes'), may hold values from 0 to 1
- tile_count: int32 [16, 5], P('nodes'), may hold values from 3 to 6, as said below
- send_mask: int32 [16, 16, 10], P('nodes'), may hold values from 0 to 1, as said below
Outputs:
- layer_out: float32 [512, 4096], P('feat', 'nodes')
- feat_grad: float32 [4096, 768], P(('nodes', 'feat'))
- rel_grad: float32 [5, 512, 768], P(None, 'feat')
- self_grad: float32 [512, 768], P('feat')
The draws below stay inside these ranges and needn't reach their ends.
Inputs may be any that keep to these rules, and one draw needn't show every extreme that they name: `tile_count`: every draw has some partition and relation with 6 live tiles. For a live tile (p, r, t), send_mask[tile_peer[p, r, t], p] holds more than tile_slot[p, r, t] ones, and the named slot's column lies in relation r's columns r * 2 to r * 2 + 1; the live tiles of a partition name distinct slots. Entries of tiles that are not live are arbitrary within the range. `tile_peer`: entries of tiles that are not live are arbitrary within the range. `send_mask`: each sending and receiving pair of partitions has at most 2 ones, and 2 are reached in every draw; every one is named by exactly one live tile.
All inputs are finite; a program needn't handle non-finite values.
Results may differ from the reference program's by a relative error of at most 0.0003.
Values sent between devices are 32-bit elements; how exact they have to be, the bound alone decides.
A program may use at most 128 MiB of HBM per device.

```python
import jax
import jax.numpy as jnp
from jax import lax

IN = 768
OUT = 512
R = 5
TILE = 128
CAP = 2
NPART = 16
NODES = 4096
BLOCKS = 2
MAXT = 6


def layout(key):
    key_count, key_offset, key_perm, key_base, key_padpeer, key_padslot = jax.random.split(key, 6)
    counts = jax.random.randint(key_count, (NPART, R), MAXT // 2, MAXT + 1)
    offset = jax.random.randint(key_offset, (), 0, R)
    part_ids = jnp.arange(NPART, dtype=jnp.int32)[:, None]
    rel_ids = jnp.arange(R, dtype=jnp.int32)[None, :]
    counts = jnp.where((part_ids + rel_ids + offset) % R == 0, MAXT, counts).astype(jnp.int32)
    total_slots = NPART * CAP

    def arrange(one_key):
        permuted = jax.random.permutation(one_key, total_slots).astype(jnp.int32)
        first = permuted[0]
        partner = first // CAP * CAP + (first % CAP + 1) % CAP
        found_at = jnp.argmax(permuted == partner)
        second = permuted[1]
        permuted = permuted.at[found_at].set(second)
        return permuted.at[1].set(partner)
    perms = jax.vmap(arrange)(jax.random.split(key_perm, NPART))
    living = (jnp.arange(MAXT, dtype=jnp.int32)[None, None, :] < counts[:, :, None]).reshape(NPART, R * MAXT)
    live_rank = jnp.clip(jnp.cumsum(living.astype(jnp.int32), axis=1) - 1, 0, total_slots - 1)
    live_pos = jnp.take_along_axis(perms, live_rank, axis=1)
    pad_pos = jax.random.randint(key_padpeer, (NPART, R * MAXT), 0, total_slots)
    position = jnp.where(living, live_pos, pad_pos).astype(jnp.int32)
    peers = position // CAP
    within = position % CAP
    block_base = jax.random.randint(key_base, (NPART, NPART), 0, BLOCKS)
    chosen_base = jnp.take_along_axis(block_base, peers, axis=1)
    blocks = (chosen_base + within) % BLOCKS
    relation = jnp.repeat(jnp.arange(R, dtype=jnp.int32), MAXT)[None, :]
    column = relation * BLOCKS + blocks
    same_pair = (peers[:, :, None] == peers[:, None, :]) & living[:, None, :]
    smaller = column[:, None, :] < column[:, :, None]
    live_slot = jnp.sum((same_pair & smaller).astype(jnp.int32), axis=2)
    pad_slot = jax.random.randint(key_padslot, (NPART, R * MAXT), 0, CAP)
    slots = jnp.where(living, live_slot, pad_slot).astype(jnp.int32)
    peer_hot = ((peers[:, :, None] == jnp.arange(NPART, dtype=jnp.int32)[None, None, :]) & living[:, :, None]).astype(jnp.int32)
    col_hot = (column[:, :, None] == jnp.arange(R * BLOCKS, dtype=jnp.int32)[None, None, :]).astype(jnp.int32)
    needed = jnp.einsum('ptq,ptc->pqc', peer_hot, col_hot)
    send_mask = jnp.transpose(needed, (1, 0, 2)).astype(jnp.int32)
    return (counts, peers.reshape(NPART, R, MAXT), slots.reshape(NPART, R, MAXT), send_mask)


def draw_tile_peer(key, part):
    return layout(key)[1]


def draw_tile_slot(key, part):
    return layout(key)[2]


def draw_tile_count(key, part):
    return layout(key)[0]


def draw_send_mask(key, part):
    return layout(key)[3]


def place_ends(entries, own_key, least, top_value):
    longest = entries.shape.index(max(entries.shape))
    spots = []
    for shift in (0, 1):
        where = [jax.random.randint(jax.random.fold_in(own_key, axis), (), 0, length) for axis, length in enumerate(entries.shape)]
        where[longest] = (where[longest] + shift) % entries.shape[longest]
        spots.append(tuple(where))
    return entries.at[spots[0]].set(least).at[spots[1]].set(top_value)


def shard_levels(own_key, shape, shards, low, top_value):
    factor_of, own = 1.0, jax.random.fold_in(own_key, 6)
    for dim, blocks in shards:
        draws = jnp.exp(jax.random.uniform(jax.random.fold_in(own, dim), (blocks,), jnp.float32, low / len(shards), top_value / len(shards)))
        factor_of = factor_of * jnp.repeat(draws, shape[dim] // blocks).reshape([-1 if axis == dim else 1 for axis in range(len(shape))])
    return factor_of


def noise(rng, extent, scale, most, cuts=(), held_as=jnp.bfloat16):
    result = jax.random.normal(rng, extent, jnp.float32) * scale
    if len(cuts) > 0:
        result = shard_levels(rng, extent, cuts, -0.22, 0.18) * result
    return jnp.clip(result, min=-most, max=most).astype(held_as)


def setup_inputs(seed: int = 0) -> dict:
    streams_of = jax.random.split(jax.random.key(seed), 11)
    node_feats = noise(streams_of[0], (NODES, IN), 1.0, 6.0, ((0, 32),), jnp.float32)
    rel_weights = noise(streams_of[1], (R, OUT, IN), IN ** -0.5, 0.21875, ((1, 2),), jnp.float32)
    self_weight = noise(streams_of[2], (OUT, IN), IN ** -0.5, 0.21875, ((0, 2),), jnp.float32)
    cotangent = noise(streams_of[3], (OUT, NODES), 1.0, 6.0, ((0, 2), (1, 16)), jnp.float32)
    tile_values = jnp.clip(0.049804688 * jax.random.uniform(streams_of[4], (NPART, R, MAXT, TILE, TILE), jnp.float32) ** shard_levels(streams_of[4], (NPART, R, MAXT, TILE, TILE), ((0, 16),), -0.2, 0.2), 0.0, 0.049804688).astype(jnp.bfloat16)
    tile_peer = draw_tile_peer(jax.random.fold_in(streams_of[10], 71), 0)
    tile_slot = draw_tile_slot(jax.random.fold_in(streams_of[10], 71), 0)
    tile_target = place_ends(jax.random.randint(streams_of[7], (NPART, R, MAXT), 0, BLOCKS), jax.random.fold_in(streams_of[7], 1), 0, BLOCKS - 1).astype(jnp.int32)
    tile_count = draw_tile_count(jax.random.fold_in(streams_of[10], 71), 0)
    send_mask = draw_send_mask(jax.random.fold_in(streams_of[10], 71), 0)
    return dict(node_feats=node_feats, rel_weights=rel_weights, self_weight=self_weight, cotangent=cotangent, tile_values=tile_values, tile_peer=tile_peer, tile_slot=tile_slot, tile_target=tile_target, tile_count=tile_count, send_mask=send_mask)


def forward(node_feats, rel_weights, self_weight, tile_values, tile_peer, tile_slot, tile_target, tile_count, send_mask):
    highest = lax.Precision.HIGHEST
    hidden = jnp.einsum('rfi,ni->rfn', rel_weights, node_feats, precision=highest)
    blocked = hidden.reshape(R, OUT, NPART * BLOCKS, TILE)
    columns = jnp.arange(R * BLOCKS, dtype=jnp.int32)
    positions = jnp.arange(MAXT, dtype=jnp.int32)
    targets = jnp.arange(BLOCKS, dtype=jnp.int32)

    def partition(index):
        peers = tile_peer[index]
        slots = tile_slot[index]
        mask_rows = send_mask[peers, index]
        slot_rank = (jnp.cumsum(mask_rows, axis=2) - 1).astype(jnp.int32)
        matched = (mask_rows == 1) & (slot_rank == slots[:, :, None])
        column = lax.optimization_barrier(jnp.sum(jnp.where(matched, columns[None, None, :], 0), axis=2)).astype(jnp.int32)
        alive = jnp.any(matched, axis=2) & (positions[None, :] < tile_count[index][:, None])
        relation = (column // BLOCKS).astype(jnp.int32)
        source = (peers * BLOCKS + column % BLOCKS).astype(jnp.int32)
        pieces = blocked[relation, :, source, :]
        pieces = pieces * alive[:, :, None, None].astype(jnp.float32)
        weights = tile_values[index].astype(jnp.float32)
        contrib = jnp.einsum('rtfu,rtvu->rtfv', pieces, weights, precision=highest)
        chooser = (tile_target[index][:, :, None] == targets[None, None, :]).astype(jnp.float32)
        return jnp.einsum('rtb,rtfv->fbv', chooser, contrib, precision=highest)
    summed = lax.map(partition, jnp.arange(NPART, dtype=jnp.int32))
    summed = summed.transpose(1, 0, 2, 3).reshape(OUT, NODES)
    return summed + jnp.einsum('fi,ni->fn', self_weight, node_feats, precision=highest)

def reference(node_feats, rel_weights, self_weight, cotangent, tile_values, tile_peer, tile_slot, tile_target, tile_count, send_mask):

    def layer(feats, weights, self_proj):
        return forward(feats, weights, self_proj, tile_values, tile_peer, tile_slot, tile_target, tile_count, send_mask)
    layer_out, pullback = jax.vjp(layer, node_feats, rel_weights, self_weight)
    feat_grad, rel_part, self_part = pullback(cotangent)
    factor = float(NODES) ** (-0.5)
    return (layer_out, feat_grad, rel_part * factor, self_part * factor)
```

```python
import functools

import jax
import jax.numpy as jnp
from jax import lax
from jax.experimental import pallas as pl
from jax.experimental.pallas import tpu as pltpu
from jax.sharding import PartitionSpec as P

TILE = 128
CAP = 2


def slot_exchange(
    node_feats,
    rel_weights,
    self_weight,
    cotangent,
    tile_values,
    tile_peer,
    tile_slot,
    tile_target,
    tile_count,
    send_mask,
):
    highest = lax.Precision.HIGHEST
    relations = rel_weights.shape[0]
    out_share = rel_weights.shape[1]
    part_rows = cotangent.shape[1]
    blocks = part_rows // TILE
    parts = lax.axis_size("nodes")
    slot_steps = tile_values.shape[2]
    combined = relations * blocks
    gathered = lax.all_gather(node_feats, "feat", axis=0, tiled=True)
    hidden = jnp.einsum("rfi,ni->rfn", rel_weights, gathered, precision=highest)
    self_part = jnp.einsum("fi,ni->fn", self_weight, gathered, precision=highest)
    hidden_blocks = (
        hidden.reshape(relations, out_share, blocks, TILE)
        .transpose(0, 2, 1, 3)
        .reshape(combined, out_share, TILE)
    )
    mask_rows = send_mask[0]
    slot_rank = jnp.cumsum(mask_rows, axis=1) - 1
    slot_ids = jnp.arange(CAP, dtype=jnp.int32)
    chooser = (
        (mask_rows[:, :, None] == 1) & (slot_rank[:, :, None] == slot_ids[None, None, :])
    ).astype(jnp.float32)
    outgoing = jnp.einsum("pcs,cfk->psfk", chooser, hidden_blocks, precision=highest)
    arrived = lax.all_to_all(outgoing, "nodes", split_axis=0, concat_axis=0, tiled=True)
    position = (tile_peer[0] * CAP + tile_slot[0]).reshape(-1)
    alive = (
        (jnp.arange(slot_steps, dtype=jnp.int32)[None, :] < tile_count[0][:, None])
        .reshape(-1)
        .astype(jnp.float32)
    )
    pieces = arrived.reshape(parts * CAP, out_share, TILE)[position] * alive[:, None, None]
    weights = tile_values[0].reshape(relations * slot_steps, TILE, TILE)
    contrib = jnp.einsum(
        "tfu,tvu->tfv", pieces, weights, precision=highest, preferred_element_type=jnp.float32
    )
    targets = (
        tile_target[0].reshape(-1)[:, None] == jnp.arange(blocks, dtype=jnp.int32)[None, :]
    ).astype(jnp.float32)
    summed = jnp.einsum("tb,tfv->fbv", targets, contrib, precision=highest).reshape(
        out_share, part_rows
    )
    layer_out = summed + self_part
    grad_blocks = cotangent.reshape(out_share, blocks, TILE)
    picked = jnp.einsum("tb,fbv->tfv", targets, grad_blocks, precision=highest)
    returned = jnp.einsum(
        "tfv,tvu->tfu", picked, weights, precision=highest, preferred_element_type=jnp.float32
    )
    placing = (position[:, None] == jnp.arange(parts * CAP, dtype=jnp.int32)[None, :]).astype(
        jnp.float32
    ) * alive[:, None]
    going_back = jnp.einsum("tq,tfu->qfu", placing, returned, precision=highest).reshape(
        parts, CAP, out_share, TILE
    )
    came_back = lax.all_to_all(going_back, "nodes", split_axis=0, concat_axis=0, tiled=True)
    source_grads = jnp.einsum("pcs,psfk->cfk", chooser, came_back, precision=highest)
    grad_hidden = (
        source_grads.reshape(relations, blocks, out_share, TILE)
        .transpose(0, 2, 1, 3)
        .reshape(relations, out_share, part_rows)
    )
    rel_local = jnp.einsum("rfn,ni->rfi", grad_hidden, gathered, precision=highest)
    self_local = jnp.dot(cotangent, gathered, precision=highest)
    rel_total, self_total = lax.psum((rel_local, self_local), "nodes")
    factor = float(part_rows * parts) ** (-0.5)
    term = jnp.einsum("rfn,rfi->ni", grad_hidden, rel_weights, precision=highest)
    feat_grad = lax.psum_scatter(
        term + jnp.einsum("fn,fi->ni", cotangent, self_weight, precision=highest),
        "feat",
        scatter_dimension=0,
        tiled=True,
    )
    return (layer_out, feat_grad, rel_total * factor, self_total * factor)


LANES = 128
MASK_ROWS = 8
VMEM_LIMIT = 60 * 1024 * 1024
MESH = pl.DeviceIdType.MESH
STEPS = 4


def bit_of(value, weight):
    return lax.rem(lax.div(value, jnp.int32(weight)), jnp.int32(2))


def place():
    node = lax.axis_index("nodes")
    share = lax.axis_index("feat")
    bits = [bit_of(node, 8), bit_of(node, 4), bit_of(node, 2), bit_of(node, 1)]
    rank = bits[0] + 2 * bits[1] + 4 * bits[2] + 8 * bits[3]
    partners = [
        (node + weight * (1 - 2 * bit), share) for weight, bit in zip((8, 4, 2, 1), bits)
    ]
    across = (node, 1 - share)
    return rank, bits, share, partners, across


def rank_of(node):
    return node // 8 % 2 + 2 * (node // 4 % 2) + 4 * (node // 2 % 2) + 8 * (node % 2)


def greet(devices):
    barrier = pltpu.get_barrier_semaphore()
    for device in devices:
        pl.semaphore_signal(barrier, inc=1, device_id=device, device_id_type=MESH)
    pl.semaphore_wait(barrier, len(devices))


class Sender:
    def __init__(self, send_sems, recv_sems):
        self.send_sems, self.recv_sems, self.used, self.copies = send_sems, recv_sems, 0, []

    def start(self, source, target, device):
        copy = pltpu.make_async_remote_copy(
            src_ref=source,
            dst_ref=target,
            send_sem=self.send_sems.at[self.used],
            recv_sem=self.recv_sems.at[self.used],
            device_id=device,
            device_id_type=MESH,
        )
        self.used += 1
        self.copies.append(copy)
        copy.start()
        return copy

    def finish(self):
        for copy in self.copies:
            copy.wait_send()


def rows(start, count):
    return pl.ds(pl.multiple_of(start, 8), count)


def columns(start, count):
    return pl.ds(pl.multiple_of(start, LANES), count)


def gather_kernel(
    feats, rel_weights, self_weight, cotangent, mask, gathered, got_weights, got_cotangent,
    send_sems, recv_sems, own_sems,
):
    rank, bits, share, partners, across = place()
    core = bits[3]
    sibling = partners[3]
    chunks = gathered.shape[0]
    half = chunks * LANES
    seg = gathered.shape[1] // 16
    relations = rel_weights.shape[0]
    own_rows = feats.shape[0]
    base = rank * seg
    own = []
    for k in range(chunks):
        for count, (source, target) in enumerate(
            (
                (
                    feats.at[:, columns(share * half + k * LANES, LANES)],
                    gathered.at[k, rows(base + share * own_rows, own_rows)],
                ),
                (mask, gathered.at[k, rows(base + 2 * own_rows, MASK_ROWS)]),
            )
        ):
            copy = pltpu.make_async_copy(source, target, own_sems.at[2 * k + count])
            copy.start()
            own.append(copy)
    greet(partners + [across])
    sender = Sender(send_sems, recv_sems)
    far = (1 - share) * half
    crossing = [
        sender.start(
            feats.at[:, columns(far + k * LANES, LANES)],
            gathered.at[k, rows(base + share * own_rows, own_rows)],
            across,
        )
        for k in range(chunks)
    ]
    cotangent_copy = sender.start(cotangent, got_cotangent, across)
    pairs = (relations + 1) // 2
    lower = [
        sender.start(
            rel_weights.at[core * (pairs - 1) + j, :, columns(far, half)],
            got_weights.at[core * (pairs - 1) + j],
            across,
        )
        for j in range(pairs - 1)
    ]
    weight_rows = rel_weights.shape[1] // 2
    lower.append(
        sender.start(
            rel_weights.at[relations - 1, rows(core * weight_rows, weight_rows), columns(far, half)],
            got_weights.at[relations - 1, rows(core * weight_rows, weight_rows)],
            across,
        )
    )
    lower.append(
        sender.start(
            self_weight.at[rows(core * weight_rows, weight_rows), columns(far, half)],
            got_weights.at[relations, rows(core * weight_rows, weight_rows)],
            across,
        )
    )
    for copy in own:
        copy.wait()
    last = list(crossing)
    for wave in range(chunks + STEPS):
        for k in range(chunks):
            step = wave - k
            if step < 0 or step > STEPS:
                continue
            last[k].wait_recv()
            if step == STEPS:
                continue
            size = 1 << step
            held = gathered.at[k, rows(lax.div(rank, jnp.int32(size)) * (size * seg), size * seg)]
            last[k] = sender.start(held, held, partners[step])
    forwarded = []
    for j, copy in enumerate(lower):
        copy.wait_recv()
        if j < pairs - 1:
            block = got_weights.at[core * (pairs - 1) + j]
        else:
            block = got_weights.at[j + pairs - 1, rows(core * weight_rows, weight_rows)]
        forwarded.append(sender.start(block, block, sibling))
    cotangent_copy.wait_recv()
    for copy in forwarded:
        copy.wait_recv()
    sender.finish()


def parts_of(value):
    high = value.astype(jnp.bfloat16)
    return high, (value - high.astype(jnp.float32)).astype(jnp.bfloat16)


def product(left, right, dims):
    def one(a, b):
        return lax.dot_general(a, b, (dims, ((), ())), preferred_element_type=jnp.float32)

    return one(left[0], right[0]) + (one(left[0], right[1]) + one(left[1], right[0]))


def exact_product(left, right, dims):
    high, low = parts_of(right)

    def one(b):
        return lax.dot_general(left, b, (dims, ((), ())), preferred_element_type=jnp.float32)

    return one(high) + one(low)


def compute_kernel(
    counts, ranks, blocks, targets, own_rank, tiles, gathered, near_weights, far_weights,
    near_cotangent, far_cotangent, near_out, far_out, feat_parts, rel_parts, mixed, mixed_grad,
):
    relations, slots = ranks.shape
    chunks = gathered.shape[0]
    part_rows = near_cotangent.shape[1]
    seg = gathered.shape[1] // 16
    near = parts_of(near_cotangent[...])
    far = parts_of(far_cotangent[...])
    near_t = parts_of(near_cotangent[...].T)
    far_t = parts_of(far_cotangent[...].T)
    feat_parts[...] = jnp.zeros_like(feat_parts)
    share_rows = near_cotangent.shape[0] // 16
    near_out[...] = jnp.zeros_like(near_out)
    far_out[...] = jnp.zeros_like(far_out)

    def weight_parts(r):
        return parts_of(near_weights[r]), parts_of(far_weights[r])

    @pl.loop(0, relations + 1)
    def _(r):
        @pl.when(r < relations)
        def _():
            mixed[...] = jnp.zeros_like(mixed)

            @pl.loop(0, counts[lax.min(r, relations - 1)])
            def _(t):
                start = ranks[r, t] * seg + blocks[r, t] * TILE
                piece = jnp.concatenate(
                    [gathered[k, rows(start, TILE), :] for k in range(chunks)], axis=1
                )
                there = rows(targets[r, t] * TILE, TILE)
                mixed[there, :] += exact_product(tiles[r * slots + t], piece, ((1,), (0,)))

        own_start = own_rank[0] * seg

        @pl.when(r == relations)
        def _():
            for k in range(chunks):
                mixed[:, k * LANES : (k + 1) * LANES] = gathered[k, rows(own_start, part_rows), :]

        near_w, far_w = weight_parts(r)
        z = parts_of(mixed[...])
        near_out[...] += product(near_w, z, ((1,), (1,)))
        far_out[...] += product(far_w, z, ((1,), (1,)))
        for which, grad in enumerate((near, far)):
            result = product(grad, z, ((1,), (0,)))
            for q in range(16):
                for k in range(chunks):
                    rel_parts[
                        k, rows(q * 2 * 6 * share_rows + which * 6 * share_rows + r * share_rows, share_rows), :
                    ] = result[q * share_rows : (q + 1) * share_rows, k * LANES : (k + 1) * LANES]
        mixed_grad[...] = product(near_t, near_w, ((1,), (0,))) + product(
            far_t, far_w, ((1,), (0,))
        )

        @pl.when(r < relations)
        def _():
            @pl.loop(0, counts[lax.min(r, relations - 1)])
            def _(t):
                start = ranks[r, t] * part_rows + blocks[r, t] * TILE
                there = rows(targets[r, t] * TILE, TILE)
                back = exact_product(tiles[r * slots + t], mixed_grad[there, :], ((0,), (0,)))
                for k in range(chunks):
                    feat_parts[k, rows(start, TILE), :] += back[:, k * LANES : (k + 1) * LANES]

        @pl.when(r == relations)
        def _():
            for k in range(chunks):
                feat_parts[k, rows(own_rank[0] * part_rows, part_rows), :] += mixed_grad[
                    :, k * LANES : (k + 1) * LANES
                ]


def add_rows(target, target_start, source, source_start, count):
    block = 64

    def body(i, carry):
        there = rows(target_start + i * block, block)
        target[there, :] = target[there, :] + source[rows(source_start + i * block, block), :]
        return carry

    lax.fori_loop(0, count // block, body, 0)


def reduce_kernel(
    feat_parts, rel_parts, far_out, rel_total, feat_total, got_out,
    feat_sums, rel_sums, send_sems, recv_sems, own_sems,
):
    rank, bits, share, partners, across = place()
    chunks = feat_parts.shape[0]
    feat_seg = feat_parts.shape[1] // 16
    rel_seg = rel_parts.shape[1] // 16
    own_rows = feat_seg // 2
    part = rel_seg // 2
    greet(partners + [across])
    sender = Sender(send_sems, recv_sems)
    out_copy = sender.start(far_out, got_out, across)
    local_copies = []

    def chain(kind, k):
        inputs, sums, seg = (
            (rel_parts, rel_sums, rel_seg) if kind == "rel" else (feat_parts, feat_sums, feat_seg)
        )
        copy = None
        for step in (3, 2, 1, 0, -1):
            if copy is not None:
                copy.wait_recv()
                size = 1 << (step + 1)
                mine = size * seg * bit_of(rank, size)
                if step == 2:
                    add_rows(
                        sums.at[k], (size - 1) * seg, inputs.at[k],
                        lax.div(rank, jnp.int32(8)) * (8 * seg), size * seg,
                    )
                else:
                    add_rows(
                        sums.at[k], (size - 1) * seg, sums.at[k],
                        (2 * size - 1) * seg + mine, size * seg,
                    )
            if step < 0:
                break
            size = 1 << step
            other = 1 - bit_of(rank, size)
            if step == 3:
                source = inputs.at[k, rows(other * (8 * seg), 8 * seg)]
            else:
                source = sums.at[
                    k, rows((2 * size - 1) * seg + other * (size * seg), size * seg)
                ]
            copy = sender.start(
                source, sums.at[k, rows((size - 1) * seg, size * seg)], partners[step]
            )
            yield
        where = share * chunks + k
        if kind == "feat":
            cross = sender.start(
                sums.at[k, rows((1 - share) * own_rows, own_rows)], feat_total.at[where], across
            )
            local = pltpu.make_async_copy(
                sums.at[k, rows(share * own_rows, own_rows)],
                feat_total.at[where],
                own_sems.at[chunks + k],
            )
            local.start()
            local_copies.append(local)
            yield
            cross.wait_recv()
            return
        cross = sender.start(
            sums.at[k, pl.ds(part, part)], rel_total.at[where, rows(rank * part, part)], across
        )
        local = pltpu.make_async_copy(
            sums.at[k, pl.ds(0, part)],
            rel_total.at[where, rows(rank * part, part)],
            own_sems.at[k],
        )
        local.start()
        local.wait()
        waiting = [None, cross]
        for wave in range(STEPS + 2):
            for piece in range(2):
                step = wave - piece
                if step < 0 or step > STEPS:
                    continue
                if waiting[piece] is not None:
                    waiting[piece].wait_recv()
                if step == STEPS:
                    continue
                size = 1 << step
                index = (share if piece == 0 else 1 - share) * chunks + k
                held = rel_total.at[
                    index, rows(lax.div(rank, jnp.int32(size)) * (size * part), size * part)
                ]
                waiting[piece] = sender.start(held, held, partners[step])
            yield

    chains = [chain("rel", k) for k in range(chunks)] + [chain("feat", k) for k in range(chunks)]
    active = []
    while chains or active:
        if chains:
            active.append(chains.pop(0))
        for one in list(active):
            if next(one, "end") == "end":
                active.remove(one)
    out_copy.wait_recv()
    for local in local_copies:
        local.wait()
    sender.finish()


def vmem(count):
    return [pl.BlockSpec(memory_space=pltpu.VMEM)] * count


def plane_gather(
    node_feats, rel_weights, self_weight, cotangent, tile_values, tile_peer, tile_slot,
    tile_target, tile_count, send_mask,
):
    f32 = jnp.float32
    relations, out_share, features = rel_weights.shape
    part_rows = cotangent.shape[1]
    own_rows = node_feats.shape[0]
    blocks = part_rows // TILE
    parts = lax.axis_size("nodes")
    half = features // 2
    chunks = half // LANES
    slots = tile_values.shape[2]
    seg = part_rows + MASK_ROWS
    node = lax.axis_index("nodes")
    share = lax.axis_index("feat")
    mask = send_mask[0].astype(f32).reshape(-1)
    mask = jnp.pad(mask, (0, MASK_ROWS * LANES - mask.shape[0])).reshape(MASK_ROWS, LANES)
    shape = jax.ShapeDtypeStruct
    gathered, far_weights, far_cotangent = pl.pallas_call(
        gather_kernel,
        out_shape=(
            shape((chunks, parts * seg, LANES), f32),
            shape((relations + 1, out_share, half), f32),
            shape((out_share, part_rows), f32),
        ),
        in_specs=vmem(5),
        out_specs=tuple(vmem(3)),
        scratch_shapes=[
            pltpu.SemaphoreType.DMA((32,)),
            pltpu.SemaphoreType.DMA((32,)),
            pltpu.SemaphoreType.DMA((2 * chunks,)),
        ],
        compiler_params=pltpu.CompilerParams(
            collective_id=0, has_side_effects=True, vmem_limit_bytes=VMEM_LIMIT
        ),
        name="gather_nodes",
    )(node_feats, rel_weights, self_weight, cotangent, mask)
    masks = gathered[0].reshape(parts, seg, LANES)[:, part_rows:].reshape(parts, -1)
    columns_all = relations * blocks
    masks = masks[:, : parts * columns_all].reshape(parts, parts, columns_all)
    to_me = jnp.sum(
        masks * (jnp.arange(parts) == node).astype(f32)[None, :, None], axis=1
    ).astype(jnp.int32)
    peer = tile_peer[0]
    peer_rank = rank_of(peer)
    picked = jnp.sum(
        jnp.where(peer_rank[:, :, None, None] == jnp.arange(parts)[None, None, :, None], to_me, 0),
        axis=2,
    )
    order = jnp.cumsum(picked, axis=2) - 1
    found = (picked == 1) & (order == tile_slot[0][:, :, None])
    column = jnp.sum(jnp.where(found, jnp.arange(columns_all)[None, None, :], 0), axis=2)
    block = (column % blocks).astype(jnp.int32)
    near_weights = lax.dynamic_slice_in_dim(
        jnp.concatenate([rel_weights, self_weight[None]]), share * half, half, 2
    )
    own_rank = rank_of(node).astype(jnp.int32).reshape(1)
    rel_rows = (relations + 1) * out_share // parts
    smem = [pl.BlockSpec(memory_space=pltpu.SMEM)] * 5
    near_out, far_out, feat_parts, rel_parts = pl.pallas_call(
        compute_kernel,
        out_shape=(
            shape((out_share, part_rows), f32),
            shape((out_share, part_rows), f32),
            shape((chunks, parts * part_rows, LANES), f32),
            shape((chunks, parts * 2 * rel_rows, LANES), f32),
        ),
        in_specs=smem + vmem(6),
        out_specs=tuple(vmem(4)),
        scratch_shapes=[pltpu.VMEM((part_rows, half), f32), pltpu.VMEM((part_rows, half), f32)],
        compiler_params=pltpu.CompilerParams(vmem_limit_bytes=VMEM_LIMIT),
        name="local_products",
    )(
        tile_count[0], peer_rank, block, tile_target[0], own_rank,
        tile_values[0].reshape(relations * slots, TILE, TILE),
        gathered, near_weights, far_weights, cotangent, far_cotangent,
    )
    rel_total, feat_total, got_out = pl.pallas_call(
        reduce_kernel,
        out_shape=(
            shape((2 * chunks, parts * rel_rows, LANES), f32),
            shape((2 * chunks, own_rows, LANES), f32),
            shape((out_share, part_rows), f32),
        ),
        in_specs=vmem(3),
        out_specs=tuple(vmem(3)),
        scratch_shapes=[
            pltpu.VMEM((chunks, 15 * part_rows, LANES), f32),
            pltpu.VMEM((chunks, 15 * 2 * rel_rows, LANES), f32),
            pltpu.SemaphoreType.DMA((72,)),
            pltpu.SemaphoreType.DMA((72,)),
            pltpu.SemaphoreType.DMA((2 * chunks,)),
        ],
        compiler_params=pltpu.CompilerParams(
            collective_id=1, has_side_effects=True, vmem_limit_bytes=VMEM_LIMIT
        ),
        name="reduce_grads",
    )(feat_parts, rel_parts, far_out)
    layer_out = near_out + got_out
    feat_grad = feat_total.transpose(1, 0, 2).reshape(own_rows, features)
    factor = float(part_rows * parts) ** (-0.5)
    totals = rel_total.reshape(2 * chunks, parts, relations + 1, out_share // parts, LANES)
    totals = totals.transpose(2, 1, 3, 0, 4).reshape(relations + 1, out_share, features) * factor
    return (layer_out, feat_grad, totals[:relations], totals[relations])


def local(node_feats, rel_weights, self_weight, cotangent, *tiles):
    relations, out_share, features = rel_weights.shape
    parts, shares = lax.axis_size("nodes"), lax.axis_size("feat")
    fits = (
        parts == 16
        and shares == 2
        and relations == 5
        and out_share == 256
        and cotangent.shape[1] == 2 * TILE
        and features == 6 * LANES
    )
    plan = plane_gather if fits else slot_exchange
    return plan(node_feats, rel_weights, self_weight, cotangent, *tiles)


def solution(mesh):
    return jax.shard_map(
        local,
        mesh=mesh,
        in_specs=(
            P(("nodes", "feat"), None),
            P(None, "feat", None),
            P("feat", None),
            P("feat", "nodes"),
            P("nodes", None, None, None, None),
            P("nodes", None, None),
            P("nodes", None, None),
            P("nodes", None, None),
            P("nodes", None),
            P("nodes", None, None),
        ),
        out_specs=(
            P("feat", "nodes"),
            P(("nodes", "feat"), None),
            P(None, "feat", None),
            P("feat", None),
        ),
        check_vma=False,
    )
```

```python
import functools

import jax
import jax.numpy as jnp
from jax import lax
from jax.experimental import pallas as pl
from jax.experimental.pallas import tpu as pltpu
from jax.sharding import PartitionSpec as P

TILE = 128
CAP = 2


def slot_exchange(
    node_feats,
    rel_weights,
    self_weight,
    cotangent,
    tile_values,
    tile_peer,
    tile_slot,
    tile_target,
    tile_count,
    send_mask,
):
    highest = lax.Precision.HIGHEST
    relations = rel_weights.shape[0]
    out_share = rel_weights.shape[1]
    part_rows = cotangent.shape[1]
    blocks = part_rows // TILE
    parts = lax.axis_size("nodes")
    slot_steps = tile_values.shape[2]
    combined = relations * blocks
    gathered = lax.all_gather(node_feats, "feat", axis=0, tiled=True)
    hidden = jnp.einsum("rfi,ni->rfn", rel_weights, gathered, precision=highest)
    self_part = jnp.einsum("fi,ni->fn", self_weight, gathered, precision=highest)
    hidden_blocks = (
        hidden.reshape(relations, out_share, blocks, TILE)
        .transpose(0, 2, 1, 3)
        .reshape(combined, out_share, TILE)
    )
    mask_rows = send_mask[0]
    slot_rank = jnp.cumsum(mask_rows, axis=1) - 1
    slot_ids = jnp.arange(CAP, dtype=jnp.int32)
    chooser = (
        (mask_rows[:, :, None] == 1) & (slot_rank[:, :, None] == slot_ids[None, None, :])
    ).astype(jnp.float32)
    outgoing = jnp.einsum("pcs,cfk->psfk", chooser, hidden_blocks, precision=highest)
    arrived = lax.all_to_all(outgoing, "nodes", split_axis=0, concat_axis=0, tiled=True)
    position = (tile_peer[0] * CAP + tile_slot[0]).reshape(-1)
    alive = (
        (jnp.arange(slot_steps, dtype=jnp.int32)[None, :] < tile_count[0][:, None])
        .reshape(-1)
        .astype(jnp.float32)
    )
    pieces = arrived.reshape(parts * CAP, out_share, TILE)[position] * alive[:, None, None]
    weights = tile_values[0].reshape(relations * slot_steps, TILE, TILE)
    contrib = jnp.einsum(
        "tfu,tvu->tfv", pieces, weights, precision=highest, preferred_element_type=jnp.float32
    )
    targets = (
        tile_target[0].reshape(-1)[:, None] == jnp.arange(blocks, dtype=jnp.int32)[None, :]
    ).astype(jnp.float32)
    summed = jnp.einsum("tb,tfv->fbv", targets, contrib, precision=highest).reshape(
        out_share, part_rows
    )
    layer_out = summed + self_part
    grad_blocks = cotangent.reshape(out_share, blocks, TILE)
    picked = jnp.einsum("tb,fbv->tfv", targets, grad_blocks, precision=highest)
    returned = jnp.einsum(
        "tfv,tvu->tfu", picked, weights, precision=highest, preferred_element_type=jnp.float32
    )
    placing = (position[:, None] == jnp.arange(parts * CAP, dtype=jnp.int32)[None, :]).astype(
        jnp.float32
    ) * alive[:, None]
    going_back = jnp.einsum("tq,tfu->qfu", placing, returned, precision=highest).reshape(
        parts, CAP, out_share, TILE
    )
    came_back = lax.all_to_all(going_back, "nodes", split_axis=0, concat_axis=0, tiled=True)
    source_grads = jnp.einsum("pcs,psfk->cfk", chooser, came_back, precision=highest)
    grad_hidden = (
        source_grads.reshape(relations, blocks, out_share, TILE)
        .transpose(0, 2, 1, 3)
        .reshape(relations, out_share, part_rows)
    )
    rel_local = jnp.einsum("rfn,ni->rfi", grad_hidden, gathered, precision=highest)
    self_local = jnp.dot(cotangent, gathered, precision=highest)
    rel_total, self_total = lax.psum((rel_local, self_local), "nodes")
    factor = float(part_rows * parts) ** (-0.5)
    term = jnp.einsum("rfn,rfi->ni", grad_hidden, rel_weights, precision=highest)
    feat_grad = lax.psum_scatter(
        term + jnp.einsum("fn,fi->ni", cotangent, self_weight, precision=highest),
        "feat",
        scatter_dimension=0,
        tiled=True,
    )
    return (layer_out, feat_grad, rel_total * factor, self_total * factor)


LANES = 128
MASK_ROWS = 8
VMEM_LIMIT = 60 * 1024 * 1024
MESH = pl.DeviceIdType.MESH
STEPS = 4


def bit_of(value, weight):
    return lax.rem(lax.div(value, jnp.int32(weight)), jnp.int32(2))


def place():
    node = lax.axis_index("nodes")
    share = lax.axis_index("feat")
    bits = [bit_of(node, 8), bit_of(node, 4), bit_of(node, 2), bit_of(node, 1)]
    rank = bits[0] + 2 * bits[1] + 4 * bits[2] + 8 * bits[3]
    partners = [
        (node + weight * (1 - 2 * bit), share) for weight, bit in zip((8, 4, 2, 1), bits)
    ]
    across = (node, 1 - share)
    return rank, bits, share, partners, across


def rank_of(node):
    z1, z0, y, core = (bit_of(node, weight) for weight in (8, 4, 2, 1))
    return z1 + 2 * z0 + 4 * y + 8 * core


def other_rank_of(node):
    z1, z0, y, core = (bit_of(node, weight) for weight in (8, 4, 2, 1))
    return z1 + 2 * y + 4 * z0 + 8 * core


def greet(devices):
    barrier = pltpu.get_barrier_semaphore()
    for device in devices:
        pl.semaphore_signal(barrier, inc=1, device_id=device, device_id_type=MESH)
    pl.semaphore_wait(barrier, len(devices))


class Sender:
    def __init__(self, send_sems, recv_sems):
        self.send_sems, self.recv_sems, self.used, self.copies = send_sems, recv_sems, 0, []

    def start(self, source, target, device):
        copy = pltpu.make_async_remote_copy(
            src_ref=source,
            dst_ref=target,
            send_sem=self.send_sems.at[self.used],
            recv_sem=self.recv_sems.at[self.used],
            device_id=device,
            device_id_type=MESH,
        )
        self.used += 1
        self.copies.append(copy)
        copy.start()
        return copy

    def finish(self):
        for copy in self.copies:
            copy.wait_send()


def rows(start, count):
    return pl.ds(pl.multiple_of(start, 8), count)


def columns(start, count):
    return pl.ds(pl.multiple_of(start, LANES), count)


def gather_kernel(
    feats, rel_weights, self_weight, cotangent, mask, gathered, got_weights, got_cotangent,
    send_sems, recv_sems, own_sems,
):
    rank, bits, share, partners, across = place()
    core = bits[3]
    sibling = partners[3]
    chunks = gathered.shape[0]
    half = chunks * LANES
    seg = gathered.shape[1] // 16
    relations = rel_weights.shape[0]
    own_rows = feats.shape[0]
    base = rank * seg
    own = []
    for k in range(chunks):
        for count, (source, target) in enumerate(
            (
                (
                    feats.at[:, columns(share * half + k * LANES, LANES)],
                    gathered.at[k, rows(base + share * own_rows, own_rows)],
                ),
                (mask, gathered.at[k, rows(base + 2 * own_rows, MASK_ROWS)]),
            )
        ):
            copy = pltpu.make_async_copy(source, target, own_sems.at[2 * k + count])
            copy.start()
            own.append(copy)
    greet(partners + [across])
    sender = Sender(send_sems, recv_sems)
    far = (1 - share) * half
    crossing = [
        sender.start(
            feats.at[:, columns(far + k * LANES, LANES)],
            gathered.at[k, rows(base + share * own_rows, own_rows)],
            across,
        )
        for k in range(chunks)
    ]
    cotangent_copy = sender.start(cotangent, got_cotangent, across)
    pairs = (relations + 1) // 2
    lower = [
        sender.start(
            rel_weights.at[core * (pairs - 1) + j, :, columns(far, half)],
            got_weights.at[core * (pairs - 1) + j],
            across,
        )
        for j in range(pairs - 1)
    ]
    weight_rows = rel_weights.shape[1] // 2
    lower.append(
        sender.start(
            rel_weights.at[relations - 1, rows(core * weight_rows, weight_rows), columns(far, half)],
            got_weights.at[relations - 1, rows(core * weight_rows, weight_rows)],
            across,
        )
    )
    lower.append(
        sender.start(
            self_weight.at[rows(core * weight_rows, weight_rows), columns(far, half)],
            got_weights.at[relations, rows(core * weight_rows, weight_rows)],
            across,
        )
    )
    for copy in own:
        copy.wait()

    def held(start, count):
        return rows(start * seg, count * seg)

    def send(k, start, count, step):
        block = gathered.at[k, held(start, count)]
        return sender.start(block, block, partners[step])

    def forward(j):
        lower[j].wait_recv()
        if j < pairs - 1:
            block = got_weights.at[core * (pairs - 1) + j]
        else:
            block = got_weights.at[j + pairs - 1, rows(core * weight_rows, weight_rows)]
        forwarded.append(sender.start(block, block, sibling))

    forwarded = []
    first, first_other = rank, rank + 1 - 2 * bits[0]
    second = rank - bits[0]
    second_other = second + 2 - 4 * bits[1]
    third = second - 2 * bits[1]
    third_other = third + 4 - 8 * bits[2]
    by_z1, by_z0, by_y, by_core = [], [], [], []
    for k in range(chunks):
        crossing[k].wait_recv()
        by_z1.append(send(k, first, 1, 0))
        by_y.append([send(k, first, 1, 2)])
    for k in range(chunks):
        by_z1[k].wait_recv()
        by_z0.append(send(k, second, 2, 1))
        by_y[k].append(send(k, first_other, 1, 2))
    for k in range(chunks):
        by_z0[k].wait_recv()
        by_y[k].append(send(k, second_other, 2, 2))
        by_core.append(send(k, third, 4, 3))
    for k in range(chunks):
        for copy in by_y[k]:
            copy.wait_recv()
        by_core.append(send(k, third_other, 4, 3))
        forward(k)
    for j in range(chunks, len(lower)):
        forward(j)
    cotangent_copy.wait_recv()
    for copy in by_core + forwarded:
        copy.wait_recv()
    sender.finish()


def parts_of(value):
    high = value.astype(jnp.bfloat16)
    return high, (value - high.astype(jnp.float32)).astype(jnp.bfloat16)


def product(left, right, dims):
    def one(a, b):
        return lax.dot_general(a, b, (dims, ((), ())), preferred_element_type=jnp.float32)

    return one(left[0], right[0]) + (one(left[0], right[1]) + one(left[1], right[0]))


def exact_product(left, right, dims):
    high, low = parts_of(right)

    def one(b):
        return lax.dot_general(left, b, (dims, ((), ())), preferred_element_type=jnp.float32)

    return one(high) + one(low)


def compute_kernel(
    counts, peers, slot_ids, targets, me, tiles, gathered, rel_weights, self_weight, far_weights,
    near_cotangent, far_cotangent, near_out, far_out, feat_parts, rel_parts, masks, mask_sems,
):
    relations, slots = peers.shape
    chunks = gathered.shape[0]
    half = chunks * LANES
    out_share, part_rows = near_cotangent.shape
    seg = gathered.shape[1] // 16
    blocks = 2
    node, share = me[0], me[1]
    copies = [
        pltpu.make_async_copy(
            gathered.at[0, pl.ds(q * seg + part_rows, MASK_ROWS)], masks.at[q], mask_sems.at[q]
        )
        for q in range(16)
    ]
    for copy in copies:
        copy.start()
    near = parts_of(near_cotangent[...])
    far = parts_of(far_cotangent[...])
    near_t = parts_of(near_cotangent[...].T)
    far_t = parts_of(far_cotangent[...].T)
    share_rows = out_share // 16
    near_columns = columns(share * half, half)
    feat_parts[...] = jnp.zeros_like(feat_parts)
    for copy in copies:
        copy.wait()

    def feat_start(k, sender):
        return (rank_of(sender) if k == 0 else other_rank_of(sender)) * part_rows

    def project(r, z, near_w):
        far_w = parts_of(far_weights[r])
        near_part = product(near_w, z, ((1,), (1,)))
        far_part = product(far_w, z, ((1,), (1,)))
        for which, grad in enumerate((near, far)):
            result = product(grad, z, ((1,), (0,)))
            for q in range(16):
                start = (q * 2 + which) * (relations + 1) * share_rows + r * share_rows
                for k in range(chunks):
                    rel_parts[k, rows(start, share_rows), :] = result[
                        q * share_rows : (q + 1) * share_rows, k * LANES : (k + 1) * LANES
                    ]
        grad = product(near_t, near_w, ((1,), (0,))) + product(far_t, far_w, ((1,), (0,)))
        return near_part, far_part, grad

    own = jnp.concatenate(
        [gathered[k, rows(rank_of(node) * seg, part_rows), :] for k in range(chunks)], axis=1
    )
    near_part, far_part, grad = project(
        relations, parts_of(own), parts_of(self_weight[:, near_columns])
    )
    near_out[...] = near_part
    far_out[...] = far_part
    for k in range(chunks):
        feat_parts[k, rows(feat_start(k, node), part_rows), :] = grad[
            :, k * LANES : (k + 1) * LANES
        ]

    @pl.loop(0, relations)
    def _(r):
        pieces, dense, places = [], [], []
        for t in range(slots):
            peer, slot, target = peers[r, t], slot_ids[r, t], targets[r, t]
            rank = rank_of(peer)
            at = node * (relations * blocks) + r * blocks

            def marked(b):
                return masks[rank, lax.div(at + b, LANES), lax.rem(at + b, LANES)] > 0.5

            block = jnp.where(
                marked(0), jnp.where(marked(1), slot, jnp.int32(0)), jnp.int32(1)
            )
            start = rank * seg + block * TILE
            pieces.append(
                jnp.concatenate(
                    [gathered[k, rows(start, TILE), :] for k in range(chunks)], axis=1
                )
            )
            tile = tiles[r * slots + t]
            alive = t < counts[r]
            dense.append(
                jnp.concatenate(
                    [
                        tile * jnp.where(alive & (target == b), 1.0, 0.0).astype(tile.dtype)
                        for b in range(blocks)
                    ],
                    axis=0,
                )
            )
            places.append((peer, block))
        dense = jnp.concatenate(dense, axis=1)
        z = parts_of(exact_product(dense, jnp.concatenate(pieces, axis=0), ((1,), (0,))))
        near_part, far_part, grad = project(r, z, parts_of(rel_weights[r, :, near_columns]))
        near_out[...] += near_part
        far_out[...] += far_part
        back = exact_product(dense, grad, ((0,), (0,)))
        for t, (peer, block) in enumerate(places):
            for k in range(chunks):
                feat_parts[k, rows(feat_start(k, peer) + block * TILE, TILE), :] += back[
                    t * TILE : (t + 1) * TILE, k * LANES : (k + 1) * LANES
                ]


def add_rows(target, target_start, source, source_start, count):
    block = 64

    def body(i, carry):
        there = rows(target_start + i * block, block)
        target[there, :] = target[there, :] + source[rows(source_start + i * block, block), :]
        return carry

    lax.fori_loop(0, count // block, body, 0)


def reduce_kernel(
    feat_parts, rel_parts, far_out, rel_total, feat_total, got_out,
    feat_sums, rel_sums, crossed, send_sems, recv_sems, own_sems,
):
    plane_rank, bits, share, plane_partners, across = place()
    other_rank = bits[0] + 2 * bits[2] + 4 * bits[1] + 8 * bits[3]
    other_partners = [plane_partners[step] for step in (0, 2, 1, 3)]
    chunks = feat_parts.shape[0]
    feat_seg = feat_parts.shape[1] // 16
    rel_seg = rel_parts.shape[1] // 16
    own_rows = feat_seg // 2
    part = rel_seg // 2
    relations = rel_total.shape[0]
    greet(plane_partners + [across])
    sender = Sender(send_sems, recv_sems)
    out_copy = sender.start(far_out, got_out, across)
    local_copies = []

    def chain(kind, k):
        inputs, sums, seg = (
            (rel_parts, rel_sums, rel_seg) if kind == "rel" else (feat_parts, feat_sums, feat_seg)
        )
        swapped = kind == "feat" and k > 0
        rank = other_rank if swapped else plane_rank
        partners = other_partners if swapped else plane_partners
        copy = None
        for step in (3, 2, 1, 0, -1):
            if copy is not None:
                copy.wait_recv()
                size = 1 << (step + 1)
                mine = size * seg * bit_of(rank, size)
                if step == 2:
                    add_rows(
                        sums.at[k], (size - 1) * seg, inputs.at[k],
                        lax.div(rank, jnp.int32(8)) * (8 * seg), size * seg,
                    )
                else:
                    add_rows(
                        sums.at[k], (size - 1) * seg, sums.at[k],
                        (2 * size - 1) * seg + mine, size * seg,
                    )
            if step < 0:
                break
            size = 1 << step
            other = 1 - bit_of(rank, size)
            if step == 3:
                source = inputs.at[k, rows(other * (8 * seg), 8 * seg)]
            else:
                source = sums.at[
                    k, rows((2 * size - 1) * seg + other * (size * seg), size * seg)
                ]
            copy = sender.start(
                source, sums.at[k, rows((size - 1) * seg, size * seg)], partners[step]
            )
            yield
        where = columns((share * chunks + k) * LANES, LANES)
        if kind == "feat":
            cross = sender.start(
                sums.at[k, rows((1 - share) * own_rows, own_rows)],
                feat_total.at[:, where],
                across,
            )
            local = pltpu.make_async_copy(
                sums.at[k, rows(share * own_rows, own_rows)], feat_total.at[:, where],
                own_sems.at[k],
            )
            local.start()
            local_copies.append(local)
            yield
            cross.wait_recv()
            return
        cross = sender.start(sums.at[k, pl.ds(part, part)], crossed.at[k], across)
        own_share = part // relations
        own_place = rows(rank * own_share, own_share)
        for r in range(relations):
            rel_total[r, own_place, where] = sums[k, r * own_share : (r + 1) * own_share, :]
        waiting = [None, None]
        for wave in range(STEPS + 2):
            for piece in range(2):
                step = wave - piece
                if step < 0 or step > STEPS:
                    continue
                spot = share if piece == 0 else 1 - share
                there = columns((spot * chunks + k) * LANES, LANES)
                if waiting[piece] is not None:
                    waiting[piece].wait_recv()
                elif piece == 1:
                    cross.wait_recv()
                    for r in range(relations):
                        rel_total[r, own_place, there] = crossed[
                            k, r * own_share : (r + 1) * own_share, :
                        ]
                if step == STEPS:
                    continue
                size = (1 << step) * own_share
                held = rel_total.at[
                    :, rows(lax.div(rank, jnp.int32(1 << step)) * size, size), there
                ]
                waiting[piece] = sender.start(held, held, partners[step])
            yield

    chains = [chain("rel", k) for k in range(chunks)] + [chain("feat", k) for k in range(chunks)]
    for one in chains:
        next(one)
    active = []
    while chains or active:
        if chains:
            active.append(chains.pop(0))
        for one in reversed(list(active)):
            if next(one, "end") == "end":
                active.remove(one)
    out_copy.wait_recv()
    for local in local_copies:
        local.wait()
    sender.finish()


def vmem(count):
    return [pl.BlockSpec(memory_space=pltpu.VMEM)] * count


def plane_gather(
    node_feats, rel_weights, self_weight, cotangent, tile_values, tile_peer, tile_slot,
    tile_target, tile_count, send_mask,
):
    f32 = jnp.float32
    relations, out_share, features = rel_weights.shape
    part_rows = cotangent.shape[1]
    own_rows = node_feats.shape[0]
    parts = lax.axis_size("nodes")
    half = features // 2
    chunks = half // LANES
    slots = tile_values.shape[2]
    seg = part_rows + MASK_ROWS
    node = lax.axis_index("nodes")
    share = lax.axis_index("feat")
    mask = send_mask[0].astype(f32).reshape(-1)
    mask = jnp.pad(mask, (0, MASK_ROWS * LANES - mask.shape[0])).reshape(MASK_ROWS, LANES)
    shape = jax.ShapeDtypeStruct
    gathered, far_weights, far_cotangent = pl.pallas_call(
        gather_kernel,
        out_shape=(
            shape((chunks, parts * seg, LANES), f32),
            shape((relations + 1, out_share, half), f32),
            shape((out_share, part_rows), f32),
        ),
        in_specs=vmem(5),
        out_specs=tuple(vmem(3)),
        scratch_shapes=[
            pltpu.SemaphoreType.DMA((40,)),
            pltpu.SemaphoreType.DMA((40,)),
            pltpu.SemaphoreType.DMA((2 * chunks,)),
        ],
        compiler_params=pltpu.CompilerParams(
            collective_id=0, has_side_effects=True, vmem_limit_bytes=VMEM_LIMIT
        ),
        name="gather_nodes",
    )(node_feats, rel_weights, self_weight, cotangent, mask)
    me = jnp.stack([node, share]).astype(jnp.int32)
    rel_rows = (relations + 1) * out_share // parts
    smem = [pl.BlockSpec(memory_space=pltpu.SMEM)] * 5
    near_out, far_out, feat_parts, rel_parts = pl.pallas_call(
        compute_kernel,
        out_shape=(
            shape((out_share, part_rows), f32),
            shape((out_share, part_rows), f32),
            shape((chunks, parts * part_rows, LANES), f32),
            shape((chunks, parts * 2 * rel_rows, LANES), f32),
        ),
        in_specs=smem + vmem(7),
        out_specs=tuple(vmem(4)),
        scratch_shapes=[
            pltpu.SMEM((parts, MASK_ROWS, LANES), f32),
            pltpu.SemaphoreType.DMA((parts,)),
        ],
        compiler_params=pltpu.CompilerParams(vmem_limit_bytes=VMEM_LIMIT),
        name="local_products",
    )(
        tile_count[0], tile_peer[0], tile_slot[0], tile_target[0], me,
        tile_values[0].reshape(relations * slots, TILE, TILE),
        gathered, rel_weights, self_weight, far_weights, cotangent, far_cotangent,
    )
    rel_total, feat_total, got_out = pl.pallas_call(
        reduce_kernel,
        out_shape=(
            shape((relations + 1, out_share, features), f32),
            shape((own_rows, features), f32),
            shape((out_share, part_rows), f32),
        ),
        in_specs=vmem(3),
        out_specs=tuple(vmem(3)),
        scratch_shapes=[
            pltpu.VMEM((chunks, 15 * part_rows, LANES), f32),
            pltpu.VMEM((chunks, 15 * 2 * rel_rows, LANES), f32),
            pltpu.VMEM((chunks, rel_rows, LANES), f32),
            pltpu.SemaphoreType.DMA((72,)),
            pltpu.SemaphoreType.DMA((72,)),
            pltpu.SemaphoreType.DMA((2 * chunks,)),
        ],
        compiler_params=pltpu.CompilerParams(
            collective_id=1, has_side_effects=True, vmem_limit_bytes=VMEM_LIMIT
        ),
        name="reduce_grads",
    )(feat_parts, rel_parts, far_out)
    layer_out = near_out + got_out
    factor = float(part_rows * parts) ** (-0.5)
    return (layer_out, feat_total, rel_total[:relations] * factor, rel_total[relations] * factor)


def local(node_feats, rel_weights, self_weight, cotangent, *tiles):
    relations, out_share, features = rel_weights.shape
    parts, shares = lax.axis_size("nodes"), lax.axis_size("feat")
    fits = (
        parts == 16
        and shares == 2
        and relations == 5
        and out_share == 256
        and cotangent.shape[1] == 2 * TILE
        and features == 6 * LANES
    )
    plan = plane_gather if fits else slot_exchange
    return plan(node_feats, rel_weights, self_weight, cotangent, *tiles)


def solution(mesh):
    return jax.shard_map(
        local,
        mesh=mesh,
        in_specs=(
            P(("nodes", "feat"), None),
            P(None, "feat", None),
            P("feat", None),
            P("feat", "nodes"),
            P("nodes", None, None, None, None),
            P("nodes", None, None),
            P("nodes", None, None),
            P("nodes", None, None),
            P("nodes", None),
            P("nodes", None, None),
        ),
        out_specs=(
            P("feat", "nodes"),
            P(("nodes", "feat"), None),
            P(None, "feat", None),
            P("feat", None),
        ),
        check_vma=False,
    )
```

```python
import functools

import jax
import jax.numpy as jnp
from jax import lax
from jax.experimental import pallas as pl
from jax.experimental.pallas import tpu as pltpu
from jax.sharding import PartitionSpec as P

TILE = 128
CAP = 2


def slot_exchange(
    node_feats,
    rel_weights,
    self_weight,
    cotangent,
    tile_values,
    tile_peer,
    tile_slot,
    tile_target,
    tile_count,
    send_mask,
):
    highest = lax.Precision.HIGHEST
    relations = rel_weights.shape[0]
    out_share = rel_weights.shape[1]
    part_rows = cotangent.shape[1]
    blocks = part_rows // TILE
    parts = lax.axis_size("nodes")
    slot_steps = tile_values.shape[2]
    combined = relations * blocks
    gathered = lax.all_gather(node_feats, "feat", axis=0, tiled=True)
    hidden = jnp.einsum("rfi,ni->rfn", rel_weights, gathered, precision=highest)
    self_part = jnp.einsum("fi,ni->fn", self_weight, gathered, precision=highest)
    hidden_blocks = (
        hidden.reshape(relations, out_share, blocks, TILE)
        .transpose(0, 2, 1, 3)
        .reshape(combined, out_share, TILE)
    )
    mask_rows = send_mask[0]
    slot_rank = jnp.cumsum(mask_rows, axis=1) - 1
    slot_ids = jnp.arange(CAP, dtype=jnp.int32)
    chooser = (
        (mask_rows[:, :, None] == 1) & (slot_rank[:, :, None] == slot_ids[None, None, :])
    ).astype(jnp.float32)
    outgoing = jnp.einsum("pcs,cfk->psfk", chooser, hidden_blocks, precision=highest)
    arrived = lax.all_to_all(outgoing, "nodes", split_axis=0, concat_axis=0, tiled=True)
    position = (tile_peer[0] * CAP + tile_slot[0]).reshape(-1)
    alive = (
        (jnp.arange(slot_steps, dtype=jnp.int32)[None, :] < tile_count[0][:, None])
        .reshape(-1)
        .astype(jnp.float32)
    )
    pieces = arrived.reshape(parts * CAP, out_share, TILE)[position] * alive[:, None, None]
    weights = tile_values[0].reshape(relations * slot_steps, TILE, TILE)
    contrib = jnp.einsum(
        "tfu,tvu->tfv", pieces, weights, precision=highest, preferred_element_type=jnp.float32
    )
    targets = (
        tile_target[0].reshape(-1)[:, None] == jnp.arange(blocks, dtype=jnp.int32)[None, :]
    ).astype(jnp.float32)
    summed = jnp.einsum("tb,tfv->fbv", targets, contrib, precision=highest).reshape(
        out_share, part_rows
    )
    layer_out = summed + self_part
    grad_blocks = cotangent.reshape(out_share, blocks, TILE)
    picked = jnp.einsum("tb,fbv->tfv", targets, grad_blocks, precision=highest)
    returned = jnp.einsum(
        "tfv,tvu->tfu", picked, weights, precision=highest, preferred_element_type=jnp.float32
    )
    placing = (position[:, None] == jnp.arange(parts * CAP, dtype=jnp.int32)[None, :]).astype(
        jnp.float32
    ) * alive[:, None]
    going_back = jnp.einsum("tq,tfu->qfu", placing, returned, precision=highest).reshape(
        parts, CAP, out_share, TILE
    )
    came_back = lax.all_to_all(going_back, "nodes", split_axis=0, concat_axis=0, tiled=True)
    source_grads = jnp.einsum("pcs,psfk->cfk", chooser, came_back, precision=highest)
    grad_hidden = (
        source_grads.reshape(relations, blocks, out_share, TILE)
        .transpose(0, 2, 1, 3)
        .reshape(relations, out_share, part_rows)
    )
    rel_local = jnp.einsum("rfn,ni->rfi", grad_hidden, gathered, precision=highest)
    self_local = jnp.dot(cotangent, gathered, precision=highest)
    rel_total, self_total = lax.psum((rel_local, self_local), "nodes")
    factor = float(part_rows * parts) ** (-0.5)
    term = jnp.einsum("rfn,rfi->ni", grad_hidden, rel_weights, precision=highest)
    feat_grad = lax.psum_scatter(
        term + jnp.einsum("fn,fi->ni", cotangent, self_weight, precision=highest),
        "feat",
        scatter_dimension=0,
        tiled=True,
    )
    return (layer_out, feat_grad, rel_total * factor, self_total * factor)


LANES = 128
MASK_ROWS = 8
VMEM_LIMIT = 60 * 1024 * 1024
MESH = pl.DeviceIdType.MESH
STEPS = 4


def bit_of(value, weight):
    return lax.rem(lax.div(value, jnp.int32(weight)), jnp.int32(2))


def place():
    node = lax.axis_index("nodes")
    share = lax.axis_index("feat")
    bits = [bit_of(node, 8), bit_of(node, 4), bit_of(node, 2), bit_of(node, 1)]
    rank = bits[0] + 2 * bits[1] + 4 * bits[2] + 8 * bits[3]
    partners = [
        (node + weight * (1 - 2 * bit), share) for weight, bit in zip((8, 4, 2, 1), bits)
    ]
    across = (node, 1 - share)
    return rank, bits, share, partners, across


def rank_of(node):
    z1, z0, y, core = (bit_of(node, weight) for weight in (8, 4, 2, 1))
    return z1 + 2 * z0 + 4 * y + 8 * core


def greet(devices):
    barrier = pltpu.get_barrier_semaphore()
    for device in devices:
        pl.semaphore_signal(barrier, inc=1, device_id=device, device_id_type=MESH)
    pl.semaphore_wait(barrier, len(devices))


class Sender:
    def __init__(self, send_sems, recv_sems):
        self.send_sems, self.recv_sems, self.used, self.copies = send_sems, recv_sems, 0, []

    def start(self, source, target, device):
        copy = pltpu.make_async_remote_copy(
            src_ref=source,
            dst_ref=target,
            send_sem=self.send_sems.at[self.used],
            recv_sem=self.recv_sems.at[self.used],
            device_id=device,
            device_id_type=MESH,
        )
        self.used += 1
        self.copies.append(copy)
        copy.start()
        return copy

    def finish(self):
        for copy in self.copies:
            copy.wait_send()


def rows(start, count):
    return pl.ds(pl.multiple_of(start, 8), count)


def columns(start, count):
    return pl.ds(pl.multiple_of(start, LANES), count)


def gather_kernel(
    feats, rel_weights, self_weight, cotangent, mask, gathered, got_weights, got_cotangent,
    send_sems, recv_sems, own_sems,
):
    rank, bits, share, partners, across = place()
    core = bits[3]
    sibling = partners[3]
    chunks = gathered.shape[0]
    half = chunks * LANES
    seg = gathered.shape[1] // 16
    relations = rel_weights.shape[0]
    own_rows = feats.shape[0]
    base = rank * seg
    own = []
    for k in range(chunks):
        for count, (source, target) in enumerate(
            (
                (
                    feats.at[:, columns(share * half + k * LANES, LANES)],
                    gathered.at[k, rows(base + share * own_rows, own_rows)],
                ),
                (mask, gathered.at[k, rows(base + 2 * own_rows, MASK_ROWS)]),
            )
        ):
            copy = pltpu.make_async_copy(source, target, own_sems.at[2 * k + count])
            copy.start()
            own.append(copy)
    greet(partners + [across])
    sender = Sender(send_sems, recv_sems)
    far = (1 - share) * half
    crossing = [
        sender.start(
            feats.at[:, columns(far + k * LANES, LANES)],
            gathered.at[k, rows(base + share * own_rows, own_rows)],
            across,
        )
        for k in range(chunks)
    ]
    cotangent_copy = sender.start(cotangent, got_cotangent, across)
    pairs = (relations + 1) // 2
    lower = [
        sender.start(
            rel_weights.at[core * (pairs - 1) + j, :, columns(far, half)],
            got_weights.at[core * (pairs - 1) + j],
            across,
        )
        for j in range(pairs - 1)
    ]
    weight_rows = rel_weights.shape[1] // 2
    lower.append(
        sender.start(
            rel_weights.at[relations - 1, rows(core * weight_rows, weight_rows), columns(far, half)],
            got_weights.at[relations - 1, rows(core * weight_rows, weight_rows)],
            across,
        )
    )
    lower.append(
        sender.start(
            self_weight.at[rows(core * weight_rows, weight_rows), columns(far, half)],
            got_weights.at[relations, rows(core * weight_rows, weight_rows)],
            across,
        )
    )
    for copy in own:
        copy.wait()

    def held(start, count):
        return rows(start * seg, count * seg)

    def send(k, start, count, step):
        block = gathered.at[k, held(start, count)]
        return sender.start(block, block, partners[step])

    def forward(j):
        lower[j].wait_recv()
        if j < pairs - 1:
            block = got_weights.at[core * (pairs - 1) + j]
        else:
            block = got_weights.at[j + pairs - 1, rows(core * weight_rows, weight_rows)]
        forwarded.append(sender.start(block, block, sibling))

    forwarded = []
    first, first_other = rank, rank + 1 - 2 * bits[0]
    second = rank - bits[0]
    second_other = second + 2 - 4 * bits[1]
    third = second - 2 * bits[1]
    third_other = third + 4 - 8 * bits[2]
    by_z1, by_z0, by_y, by_core = [], [], [], []
    for k in range(chunks):
        crossing[k].wait_recv()
        by_z1.append(send(k, first, 1, 0))
        by_y.append([send(k, first, 1, 2)])
    for k in range(chunks):
        by_z1[k].wait_recv()
        by_z0.append(send(k, second, 2, 1))
        by_y[k].append(send(k, first_other, 1, 2))
    for k in range(chunks):
        by_z0[k].wait_recv()
        by_y[k].append(send(k, second_other, 2, 2))
        by_core.append(send(k, third, 4, 3))
    for k in range(chunks):
        for copy in by_y[k]:
            copy.wait_recv()
        by_core.append(send(k, third_other, 4, 3))
        forward(k)
    for j in range(chunks, len(lower)):
        forward(j)
    cotangent_copy.wait_recv()
    for copy in by_core + forwarded:
        copy.wait_recv()
    sender.finish()


def parts_of(value):
    high = value.astype(jnp.bfloat16)
    return high, (value - high.astype(jnp.float32)).astype(jnp.bfloat16)


def product(left, right, dims):
    def one(a, b):
        return lax.dot_general(a, b, (dims, ((), ())), preferred_element_type=jnp.float32)

    return one(left[0], right[0]) + (one(left[0], right[1]) + one(left[1], right[0]))


def exact_product(left, right, dims):
    high, low = parts_of(right)

    def one(b):
        return lax.dot_general(left, b, (dims, ((), ())), preferred_element_type=jnp.float32)

    return one(high) + one(low)


def compute_kernel(
    codes, me, tiles, gathered, rel_weights, self_weight, far_weights,
    near_cotangent, far_cotangent, near_out, far_out, feat_parts, rel_parts, masks, mask_sems,
):
    relations, slots = codes.shape
    chunks = gathered.shape[0]
    half = chunks * LANES
    out_share, part_rows = near_cotangent.shape
    seg = gathered.shape[1] // 16
    blocks = 2
    node, share = me[0], me[1]
    copies = [
        pltpu.make_async_copy(
            gathered.at[0, pl.ds(q * seg + part_rows, MASK_ROWS)], masks.at[q], mask_sems.at[q]
        )
        for q in range(16)
    ]
    for copy in copies:
        copy.start()
    near = parts_of(near_cotangent[...])
    far = parts_of(far_cotangent[...])
    near_t = parts_of(near_cotangent[...].T)
    far_t = parts_of(far_cotangent[...].T)
    share_rows = out_share // 16
    near_columns = columns(share * half, half)
    feat_parts[...] = jnp.zeros_like(feat_parts)
    for copy in copies:
        copy.wait()

    def feat_start(sender):
        return rank_of(sender) * part_rows

    def project(r, z, near_w):
        far_w = parts_of(far_weights[r])
        near_part = product(near_w, z, ((1,), (1,)))
        far_part = product(far_w, z, ((1,), (1,)))
        for which, grad in enumerate((near, far)):
            result = product(grad, z, ((1,), (0,)))
            for q in range(16):
                start = (q * 2 + which) * (relations + 1) * share_rows + r * share_rows
                for k in range(chunks):
                    rel_parts[k, rows(start, share_rows), :] = result[
                        q * share_rows : (q + 1) * share_rows, k * LANES : (k + 1) * LANES
                    ]
        grad = product(near_t, near_w, ((1,), (0,))) + product(far_t, far_w, ((1,), (0,)))
        return near_part, far_part, grad

    own = jnp.concatenate(
        [gathered[k, rows(rank_of(node) * seg, part_rows), :] for k in range(chunks)], axis=1
    )
    near_part, far_part, grad = project(
        relations, parts_of(own), parts_of(self_weight[:, near_columns])
    )
    near_out[...] = near_part
    far_out[...] = far_part
    for k in range(chunks):
        feat_parts[k, rows(feat_start(node), part_rows), :] = grad[
            :, k * LANES : (k + 1) * LANES
        ]

    @pl.loop(0, relations)
    def _(r):
        pieces, dense, places = [], [], []
        for t in range(slots):
            code = codes[r, t]
            alive, target, slot = (bit_of(code, weight) == 1 for weight in (1, 2, 4))
            peer = lax.div(code, jnp.int32(8))
            rank = rank_of(peer)
            at = node * (relations * blocks) + r * blocks

            def marked(b):
                return masks[rank, lax.div(at + b, LANES), lax.rem(at + b, LANES)] > 0.5

            block = jnp.where(
                marked(0), jnp.where(marked(1) & slot, jnp.int32(1), jnp.int32(0)), jnp.int32(1)
            )
            start = rank * seg + block * TILE
            pieces.append(
                jnp.concatenate(
                    [gathered[k, rows(start, TILE), :] for k in range(chunks)], axis=1
                )
            )
            tile = tiles[r * slots + t]
            dense.append(
                jnp.concatenate(
                    [
                        tile * jnp.where(alive & (target if b == 1 else ~target), 1.0, 0.0).astype(tile.dtype)
                        for b in range(blocks)
                    ],
                    axis=0,
                )
            )
            places.append((peer, block))
        dense = jnp.concatenate(dense, axis=1)
        z = parts_of(exact_product(dense, jnp.concatenate(pieces, axis=0), ((1,), (0,))))
        near_part, far_part, grad = project(r, z, parts_of(rel_weights[r, :, near_columns]))
        near_out[...] += near_part
        far_out[...] += far_part
        back = exact_product(dense, grad, ((0,), (0,)))
        for t, (peer, block) in enumerate(places):
            for k in range(chunks):
                feat_parts[k, rows(feat_start(peer) + block * TILE, TILE), :] += back[
                    t * TILE : (t + 1) * TILE, k * LANES : (k + 1) * LANES
                ]


def add_rows(target, target_start, source, source_start, count, block):

    def body(i, carry):
        there = rows(target_start + i * block, block)
        target[there, :] = target[there, :] + source[rows(source_start + i * block, block), :]
        return carry

    lax.fori_loop(0, count // block, body, 0)


def reduce_kernel(
    feat_parts, rel_parts, far_out, rel_total, self_total, feat_total, got_out,
    feat_sums, rel_sums, crossed, send_sems, recv_sems, own_sems,
):
    rank, bits, share, partners, across = place()
    chunks = feat_parts.shape[0]
    feat_seg = feat_parts.shape[1] // 16
    rel_seg = rel_parts.shape[1] // 16
    own_rows = feat_seg // 2
    part = rel_seg // 2
    relations = rel_total.shape[0]
    greet(partners + [across])
    sender = Sender(send_sems, recv_sems)
    out_copy = sender.start(far_out, got_out, across)
    local_copies = []

    def chain(kind, k):
        inputs, sums, seg = (
            (rel_parts, rel_sums, rel_seg) if kind == "rel" else (feat_parts, feat_sums, feat_seg)
        )
        copy = None
        for step in (3, 2, 1, 0, -1):
            if copy is not None:
                copy.wait_recv()
                size = 1 << (step + 1)
                mine = size * seg * bit_of(rank, size)
                if step == 2:
                    add_rows(
                        sums.at[k], (size - 1) * seg, inputs.at[k],
                        lax.div(rank, jnp.int32(8)) * (8 * seg), size * seg, seg,
                    )
                else:
                    add_rows(
                        sums.at[k], (size - 1) * seg, sums.at[k],
                        (2 * size - 1) * seg + mine, size * seg, seg,
                    )
            if step < 0:
                break
            size = 1 << step
            other = 1 - bit_of(rank, size)
            if step == 3:
                source = inputs.at[k, rows(other * (8 * seg), 8 * seg)]
            else:
                source = sums.at[
                    k, rows((2 * size - 1) * seg + other * (size * seg), size * seg)
                ]
            copy = sender.start(
                source, sums.at[k, rows((size - 1) * seg, size * seg)], partners[step]
            )
            yield
        where = columns((share * chunks + k) * LANES, LANES)
        if kind == "feat":
            cross = sender.start(
                sums.at[k, rows((1 - share) * own_rows, own_rows)],
                feat_total.at[:, where],
                across,
            )
            local = pltpu.make_async_copy(
                sums.at[k, rows(share * own_rows, own_rows)], feat_total.at[:, where],
                own_sems.at[k],
            )
            local.start()
            local_copies.append(local)
            yield
            cross.wait_recv()
            return
        cross = sender.start(sums.at[k, pl.ds(part, part)], crossed.at[k], across)
        own_share = part // (relations + 1)
        own_place = rows(rank * own_share, own_share)
        for r in range(relations):
            rel_total[r, own_place, where] = sums[k, r * own_share : (r + 1) * own_share, :]
        self_total[own_place, where] = sums[k, relations * own_share : part, :]
        waiting = [(), ()]
        for wave in range(STEPS + 2):
            for piece in range(2):
                step = wave - piece
                if step < 0 or step > STEPS:
                    continue
                spot = share if piece == 0 else 1 - share
                there = columns((spot * chunks + k) * LANES, LANES)
                for copy in waiting[piece]:
                    copy.wait_recv()
                if piece == 1 and step == 0:
                    cross.wait_recv()
                    for r in range(relations):
                        rel_total[r, own_place, there] = crossed[
                            k, r * own_share : (r + 1) * own_share, :
                        ]
                    self_total[own_place, there] = crossed[k, relations * own_share : part, :]
                if step == STEPS:
                    continue
                size = (1 << step) * own_share
                span = rows(lax.div(rank, jnp.int32(1 << step)) * size, size)
                waiting[piece] = [
                    sender.start(held, held, partners[step])
                    for held in (rel_total.at[:, span, there], self_total.at[span, there])
                ]
            yield

    chains = [chain("rel", k) for k in range(chunks)] + [chain("feat", k) for k in range(chunks)]
    next(chains[0])
    active = []
    while chains or active:
        if len(chains) > 1:
            next(chains[1])
        if chains:
            active.append(chains.pop(0))
        for one in reversed(list(active)):
            if next(one, "end") == "end":
                active.remove(one)
    out_copy.wait_recv()
    for local in local_copies:
        local.wait()
    sender.finish()


def vmem(count):
    return [pl.BlockSpec(memory_space=pltpu.VMEM)] * count


def plane_gather(
    node_feats, rel_weights, self_weight, cotangent, tile_values, tile_peer, tile_slot,
    tile_target, tile_count, send_mask,
):
    f32 = jnp.float32
    relations, out_share, features = rel_weights.shape
    part_rows = cotangent.shape[1]
    own_rows = node_feats.shape[0]
    parts = lax.axis_size("nodes")
    half = features // 2
    chunks = half // LANES
    slots = tile_values.shape[2]
    seg = part_rows + MASK_ROWS
    node = lax.axis_index("nodes")
    share = lax.axis_index("feat")
    mask = send_mask[0].astype(f32).reshape(-1)
    mask = jnp.pad(mask, (0, MASK_ROWS * LANES - mask.shape[0])).reshape(MASK_ROWS, LANES)
    shape = jax.ShapeDtypeStruct
    gathered, far_weights, far_cotangent = pl.pallas_call(
        gather_kernel,
        out_shape=(
            shape((chunks, parts * seg, LANES), f32),
            shape((relations + 1, out_share, half), f32),
            shape((out_share, part_rows), f32),
        ),
        in_specs=vmem(5),
        out_specs=tuple(vmem(3)),
        scratch_shapes=[
            pltpu.SemaphoreType.DMA((40,)),
            pltpu.SemaphoreType.DMA((40,)),
            pltpu.SemaphoreType.DMA((2 * chunks,)),
        ],
        compiler_params=pltpu.CompilerParams(
            collective_id=0, has_side_effects=True, vmem_limit_bytes=VMEM_LIMIT
        ),
        name="gather_nodes",
    )(node_feats, rel_weights, self_weight, cotangent, mask)
    alive = jnp.arange(slots, dtype=jnp.int32)[None, :] < tile_count[0][:, None]
    codes = tile_peer[0] * 8 + tile_slot[0] * 4 + tile_target[0] * 2 + alive.astype(jnp.int32)
    me = jnp.stack([node, share]).astype(jnp.int32)
    rel_rows = (relations + 1) * out_share // parts
    smem = [pl.BlockSpec(memory_space=pltpu.SMEM)] * 2
    near_out, far_out, feat_parts, rel_parts = pl.pallas_call(
        compute_kernel,
        out_shape=(
            shape((out_share, part_rows), f32),
            shape((out_share, part_rows), f32),
            shape((chunks, parts * part_rows, LANES), f32),
            shape((chunks, parts * 2 * rel_rows, LANES), f32),
        ),
        in_specs=smem + vmem(7),
        out_specs=tuple(vmem(4)),
        scratch_shapes=[
            pltpu.SMEM((parts, MASK_ROWS, LANES), f32),
            pltpu.SemaphoreType.DMA((parts,)),
        ],
        compiler_params=pltpu.CompilerParams(vmem_limit_bytes=VMEM_LIMIT),
        name="local_products",
    )(
        codes, me,
        tile_values[0].reshape(relations * slots, TILE, TILE),
        gathered, rel_weights, self_weight, far_weights, cotangent, far_cotangent,
    )
    rel_total, self_total, feat_total, got_out = pl.pallas_call(
        reduce_kernel,
        out_shape=(
            shape((relations, out_share, features), f32),
            shape((out_share, features), f32),
            shape((own_rows, features), f32),
            shape((out_share, part_rows), f32),
        ),
        in_specs=vmem(3),
        out_specs=tuple(vmem(4)),
        scratch_shapes=[
            pltpu.VMEM((chunks, 15 * part_rows, LANES), f32),
            pltpu.VMEM((chunks, 15 * 2 * rel_rows, LANES), f32),
            pltpu.VMEM((chunks, rel_rows, LANES), f32),
            pltpu.SemaphoreType.DMA((96,)),
            pltpu.SemaphoreType.DMA((96,)),
            pltpu.SemaphoreType.DMA((2 * chunks,)),
        ],
        compiler_params=pltpu.CompilerParams(
            collective_id=1, has_side_effects=True, vmem_limit_bytes=VMEM_LIMIT
        ),
        name="reduce_grads",
    )(feat_parts, rel_parts, far_out)
    layer_out = near_out + got_out
    factor = float(part_rows * parts) ** (-0.5)
    return (layer_out, feat_total, rel_total * factor, self_total * factor)


def local(node_feats, rel_weights, self_weight, cotangent, *tiles):
    relations, out_share, features = rel_weights.shape
    parts, shares = lax.axis_size("nodes"), lax.axis_size("feat")
    fits = (
        parts == 16
        and shares == 2
        and relations == 5
        and out_share == 256
        and cotangent.shape[1] == 2 * TILE
        and features == 6 * LANES
    )
    plan = plane_gather if fits else slot_exchange
    return plan(node_feats, rel_weights, self_weight, cotangent, *tiles)


def solution(mesh):
    return jax.shard_map(
        local,
        mesh=mesh,
        in_specs=(
            P(("nodes", "feat"), None),
            P(None, "feat", None),
            P("feat", None),
            P("feat", "nodes"),
            P("nodes", None, None, None, None),
            P("nodes", None, None),
            P("nodes", None, None),
            P("nodes", None, None),
            P("nodes", None),
            P("nodes", None, None),
        ),
        out_specs=(
            P("feat", "nodes"),
            P(("nodes", "feat"), None),
            P(None, "feat", None),
            P("feat", None),
        ),
        check_vma=False,
    )
```

```python
import functools

import jax
import jax.numpy as jnp
from jax import lax
from jax.experimental import pallas as pl
from jax.experimental.pallas import tpu as pltpu
from jax.sharding import PartitionSpec as P

TILE = 128
CAP = 2


def slot_exchange(
    node_feats,
    rel_weights,
    self_weight,
    cotangent,
    tile_values,
    tile_peer,
    tile_slot,
    tile_target,
    tile_count,
    send_mask,
):
    highest = lax.Precision.HIGHEST
    relations = rel_weights.shape[0]
    out_share = rel_weights.shape[1]
    part_rows = cotangent.shape[1]
    blocks = part_rows // TILE
    parts = lax.axis_size("nodes")
    slot_steps = tile_values.shape[2]
    combined = relations * blocks
    gathered = lax.all_gather(node_feats, "feat", axis=0, tiled=True)
    hidden = jnp.einsum("rfi,ni->rfn", rel_weights, gathered, precision=highest)
    self_part = jnp.einsum("fi,ni->fn", self_weight, gathered, precision=highest)
    hidden_blocks = (
        hidden.reshape(relations, out_share, blocks, TILE)
        .transpose(0, 2, 1, 3)
        .reshape(combined, out_share, TILE)
    )
    mask_rows = send_mask[0]
    slot_rank = jnp.cumsum(mask_rows, axis=1) - 1
    slot_ids = jnp.arange(CAP, dtype=jnp.int32)
    chooser = (
        (mask_rows[:, :, None] == 1) & (slot_rank[:, :, None] == slot_ids[None, None, :])
    ).astype(jnp.float32)
    outgoing = jnp.einsum("pcs,cfk->psfk", chooser, hidden_blocks, precision=highest)
    arrived = lax.all_to_all(outgoing, "nodes", split_axis=0, concat_axis=0, tiled=True)
    position = (tile_peer[0] * CAP + tile_slot[0]).reshape(-1)
    alive = (
        (jnp.arange(slot_steps, dtype=jnp.int32)[None, :] < tile_count[0][:, None])
        .reshape(-1)
        .astype(jnp.float32)
    )
    pieces = arrived.reshape(parts * CAP, out_share, TILE)[position] * alive[:, None, None]
    weights = tile_values[0].reshape(relations * slot_steps, TILE, TILE)
    contrib = jnp.einsum(
        "tfu,tvu->tfv", pieces, weights, precision=highest, preferred_element_type=jnp.float32
    )
    targets = (
        tile_target[0].reshape(-1)[:, None] == jnp.arange(blocks, dtype=jnp.int32)[None, :]
    ).astype(jnp.float32)
    summed = jnp.einsum("tb,tfv->fbv", targets, contrib, precision=highest).reshape(
        out_share, part_rows
    )
    layer_out = summed + self_part
    grad_blocks = cotangent.reshape(out_share, blocks, TILE)
    picked = jnp.einsum("tb,fbv->tfv", targets, grad_blocks, precision=highest)
    returned = jnp.einsum(
        "tfv,tvu->tfu", picked, weights, precision=highest, preferred_element_type=jnp.float32
    )
    placing = (position[:, None] == jnp.arange(parts * CAP, dtype=jnp.int32)[None, :]).astype(
        jnp.float32
    ) * alive[:, None]
    going_back = jnp.einsum("tq,tfu->qfu", placing, returned, precision=highest).reshape(
        parts, CAP, out_share, TILE
    )
    came_back = lax.all_to_all(going_back, "nodes", split_axis=0, concat_axis=0, tiled=True)
    source_grads = jnp.einsum("pcs,psfk->cfk", chooser, came_back, precision=highest)
    grad_hidden = (
        source_grads.reshape(relations, blocks, out_share, TILE)
        .transpose(0, 2, 1, 3)
        .reshape(relations, out_share, part_rows)
    )
    rel_local = jnp.einsum("rfn,ni->rfi", grad_hidden, gathered, precision=highest)
    self_local = jnp.dot(cotangent, gathered, precision=highest)
    rel_total, self_total = lax.psum((rel_local, self_local), "nodes")
    factor = float(part_rows * parts) ** (-0.5)
    term = jnp.einsum("rfn,rfi->ni", grad_hidden, rel_weights, precision=highest)
    feat_grad = lax.psum_scatter(
        term + jnp.einsum("fn,fi->ni", cotangent, self_weight, precision=highest),
        "feat",
        scatter_dimension=0,
        tiled=True,
    )
    return (layer_out, feat_grad, rel_total * factor, self_total * factor)


LANES = 128
MASK_ROWS = 8
MIB = 1024 * 1024
MESH = pl.DeviceIdType.MESH
STEPS = 4


def bit_of(value, weight):
    return lax.rem(lax.div(value, jnp.int32(weight)), jnp.int32(2))


def place():
    node = lax.axis_index("nodes")
    share = lax.axis_index("feat")
    bits = [bit_of(node, 8), bit_of(node, 4), bit_of(node, 2), bit_of(node, 1)]
    rank = bits[0] + 2 * bits[1] + 4 * bits[2] + 8 * bits[3]
    partners = [
        (node + weight * (1 - 2 * bit), share) for weight, bit in zip((8, 4, 2, 1), bits)
    ]
    across = (node, 1 - share)
    return rank, bits, share, partners, across


def rank_of(node):
    z1, z0, y, core = (bit_of(node, weight) for weight in (8, 4, 2, 1))
    return z1 + 2 * z0 + 4 * y + 8 * core


def greet(devices):
    barrier = pltpu.get_barrier_semaphore()
    for device in devices:
        pl.semaphore_signal(barrier, inc=1, device_id=device, device_id_type=MESH)
    pl.semaphore_wait(barrier, len(devices))


class Sender:
    def __init__(self, send_sems, recv_sems):
        self.send_sems, self.recv_sems, self.used, self.copies = send_sems, recv_sems, 0, []

    def start(self, source, target, device):
        copy = pltpu.make_async_remote_copy(
            src_ref=source,
            dst_ref=target,
            send_sem=self.send_sems.at[self.used],
            recv_sem=self.recv_sems.at[self.used],
            device_id=device,
            device_id_type=MESH,
        )
        self.used += 1
        self.copies.append(copy)
        copy.start()
        return copy

    def finish(self):
        for copy in self.copies:
            copy.wait_send()


def rows(start, count):
    return pl.ds(pl.multiple_of(start, 8), count)


def columns(start, count):
    return pl.ds(pl.multiple_of(start, LANES), count)


def gather_kernel(
    feats, rel_weights, self_weight, cotangent, mask, gathered, got_weights, got_cotangent,
    send_sems, recv_sems, own_sems,
):
    rank, bits, share, partners, across = place()
    core = bits[3]
    sibling = partners[3]
    chunks = gathered.shape[0]
    half = chunks * LANES
    seg = gathered.shape[1] // 16
    relations = rel_weights.shape[0]
    own_rows = feats.shape[0]
    base = rank * seg
    own = []
    for k in range(chunks):
        for count, (source, target) in enumerate(
            (
                (
                    feats.at[:, columns(share * half + k * LANES, LANES)],
                    gathered.at[k, rows(base + share * own_rows, own_rows)],
                ),
                (mask, gathered.at[k, rows(base + 2 * own_rows, MASK_ROWS)]),
            )
        ):
            copy = pltpu.make_async_copy(source, target, own_sems.at[2 * k + count])
            copy.start()
            own.append(copy)
    greet(partners + [across])
    sender = Sender(send_sems, recv_sems)
    far = (1 - share) * half
    crossing = [
        sender.start(
            feats.at[:, columns(far + k * LANES, LANES)],
            gathered.at[k, rows(base + share * own_rows, own_rows)],
            across,
        )
        for k in range(chunks)
    ]
    cotangent_copy = sender.start(cotangent, got_cotangent, across)
    pairs = (relations + 1) // 2
    lower = [
        sender.start(
            rel_weights.at[core * (pairs - 1) + j, :, columns(far, half)],
            got_weights.at[core * (pairs - 1) + j],
            across,
        )
        for j in range(pairs - 1)
    ]
    weight_rows = rel_weights.shape[1] // 2
    lower.append(
        sender.start(
            rel_weights.at[relations - 1, rows(core * weight_rows, weight_rows), columns(far, half)],
            got_weights.at[relations - 1, rows(core * weight_rows, weight_rows)],
            across,
        )
    )
    lower.append(
        sender.start(
            self_weight.at[rows(core * weight_rows, weight_rows), columns(far, half)],
            got_weights.at[relations, rows(core * weight_rows, weight_rows)],
            across,
        )
    )
    for copy in own:
        copy.wait()

    def held(start, count):
        return rows(start * seg, count * seg)

    def send(k, start, count, step):
        block = gathered.at[k, held(start, count)]
        return sender.start(block, block, partners[step])

    def forward(j):
        lower[j].wait_recv()
        if j < pairs - 1:
            block = got_weights.at[core * (pairs - 1) + j]
        else:
            block = got_weights.at[j + pairs - 1, rows(core * weight_rows, weight_rows)]
        forwarded.append(sender.start(block, block, sibling))

    forwarded = []
    first, first_other = rank, rank + 1 - 2 * bits[0]
    second = rank - bits[0]
    second_other = second + 2 - 4 * bits[1]
    third = second - 2 * bits[1]
    third_other = third + 4 - 8 * bits[2]
    by_z1, by_z0, by_y, by_core = [], [], [], []
    for k in range(chunks):
        crossing[k].wait_recv()
        by_z1.append(send(k, first, 1, 0))
        by_y.append([send(k, first, 1, 2)])
    for k in range(chunks):
        by_z1[k].wait_recv()
        by_z0.append(send(k, second, 2, 1))
        by_y[k].append(send(k, first_other, 1, 2))
    for k in range(chunks):
        by_z0[k].wait_recv()
        by_y[k].append(send(k, second_other, 2, 2))
        by_core.append(send(k, third, 4, 3))
    for k in range(chunks):
        for copy in by_y[k]:
            copy.wait_recv()
        by_core.append(send(k, third_other, 4, 3))
        forward(k)
    for j in range(chunks, len(lower)):
        forward(j)
    cotangent_copy.wait_recv()
    for copy in by_core + forwarded:
        copy.wait_recv()
    sender.finish()


def parts_of(value):
    high = value.astype(jnp.bfloat16)
    return high, (value - high.astype(jnp.float32)).astype(jnp.bfloat16)


def product(left, right, dims):
    def one(a, b):
        return lax.dot_general(a, b, (dims, ((), ())), preferred_element_type=jnp.float32)

    return one(left[0], right[0]) + (one(left[0], right[1]) + one(left[1], right[0]))


def exact_product(left, right, dims):
    high, low = parts_of(right)

    def one(b):
        return lax.dot_general(left, b, (dims, ((), ())), preferred_element_type=jnp.float32)

    return one(high) + one(low)


def compute_kernel(
    codes, me, tiles, gathered, rel_weights, self_weight, far_weights,
    near_cotangent, far_cotangent, near_out, far_out, feat_parts, rel_parts, masks, mask_sems,
):
    relations, slots = codes.shape
    chunks = gathered.shape[0]
    half = chunks * LANES
    out_share, part_rows = near_cotangent.shape
    seg = gathered.shape[1] // 16
    blocks = 2
    node, share = me[0], me[1]
    copies = [
        pltpu.make_async_copy(
            gathered.at[0, pl.ds(q * seg + part_rows, MASK_ROWS)], masks.at[q], mask_sems.at[q]
        )
        for q in range(16)
    ]
    for copy in copies:
        copy.start()
    near = parts_of(near_cotangent[...])
    far = parts_of(far_cotangent[...])
    near_t = parts_of(near_cotangent[...].T)
    far_t = parts_of(far_cotangent[...].T)
    share_rows = out_share // 16
    near_columns = columns(share * half, half)
    feat_parts[...] = jnp.zeros_like(feat_parts)
    for copy in copies:
        copy.wait()

    def feat_start(sender):
        return rank_of(sender) * part_rows

    def project(r, z, near_w):
        far_w = parts_of(far_weights[r])
        near_part = product(near_w, z, ((1,), (1,)))
        far_part = product(far_w, z, ((1,), (1,)))
        for which, grad in enumerate((near, far)):
            result = product(grad, z, ((1,), (0,)))
            for q in range(16):
                start = (q * 2 + which) * (relations + 1) * share_rows + r * share_rows
                for k in range(chunks):
                    rel_parts[k, rows(start, share_rows), :] = result[
                        q * share_rows : (q + 1) * share_rows, k * LANES : (k + 1) * LANES
                    ]
        grad = product(near_t, near_w, ((1,), (0,))) + product(far_t, far_w, ((1,), (0,)))
        return near_part, far_part, grad

    own = jnp.concatenate(
        [gathered[k, rows(rank_of(node) * seg, part_rows), :] for k in range(chunks)], axis=1
    )
    near_part, far_part, grad = project(
        relations, parts_of(own), parts_of(self_weight[:, near_columns])
    )
    near_out[...] = near_part
    far_out[...] = far_part
    for k in range(chunks):
        feat_parts[k, rows(feat_start(node), part_rows), :] = grad[
            :, k * LANES : (k + 1) * LANES
        ]

    @pl.loop(0, relations)
    def _(r):
        pieces, dense, places = [], [], []
        for t in range(slots):
            code = codes[r, t]
            alive, target, slot = (bit_of(code, weight) == 1 for weight in (1, 2, 4))
            peer = lax.div(code, jnp.int32(8))
            rank = rank_of(peer)
            at = node * (relations * blocks) + r * blocks

            def marked(b):
                return masks[rank, lax.div(at + b, LANES), lax.rem(at + b, LANES)] > 0.5

            block = jnp.where(
                marked(0), jnp.where(marked(1) & slot, jnp.int32(1), jnp.int32(0)), jnp.int32(1)
            )
            start = rank * seg + block * TILE
            pieces.append(
                jnp.concatenate(
                    [gathered[k, rows(start, TILE), :] for k in range(chunks)], axis=1
                )
            )
            tile = tiles[r * slots + t]
            dense.append(
                jnp.concatenate(
                    [
                        tile * jnp.where(alive & (target if b == 1 else ~target), 1.0, 0.0).astype(tile.dtype)
                        for b in range(blocks)
                    ],
                    axis=0,
                )
            )
            places.append((peer, block))
        dense = jnp.concatenate(dense, axis=1)
        z = parts_of(exact_product(dense, jnp.concatenate(pieces, axis=0), ((1,), (0,))))
        near_part, far_part, grad = project(r, z, parts_of(rel_weights[r, :, near_columns]))
        near_out[...] += near_part
        far_out[...] += far_part
        back = exact_product(dense, grad, ((0,), (0,)))
        for t, (peer, block) in enumerate(places):
            for k in range(chunks):
                feat_parts[k, rows(feat_start(peer) + block * TILE, TILE), :] += back[
                    t * TILE : (t + 1) * TILE, k * LANES : (k + 1) * LANES
                ]


def add_rows(target, target_start, source, source_start, count, block):

    def body(i, carry):
        there = rows(target_start + i * block, block)
        target[there, :] = target[there, :] + source[rows(source_start + i * block, block), :]
        return carry

    lax.fori_loop(0, count // block, body, 0)


def reduce_kernel(
    feat_parts, rel_parts, far_out, rel_total, self_total, feat_total, got_out,
    feat_sums, rel_sums, crossed, send_sems, recv_sems, own_sems,
):
    rank, bits, share, partners, across = place()
    chunks = feat_parts.shape[0]
    feat_seg = feat_parts.shape[1] // 16
    rel_seg = rel_parts.shape[1] // 16
    own_rows = feat_seg // 2
    part = rel_seg // 2
    relations = rel_total.shape[0]
    greet(partners + [across])
    sender = Sender(send_sems, recv_sems)
    out_copy = sender.start(far_out, got_out, across)
    local_copies = []

    def chain(kind, k):
        inputs, sums, seg = (
            (rel_parts, rel_sums, rel_seg) if kind == "rel" else (feat_parts, feat_sums, feat_seg)
        )
        copy = None
        for step in (3, 2, 1, 0, -1):
            if copy is not None:
                copy.wait_recv()
                size = 1 << (step + 1)
                mine = size * seg * bit_of(rank, size)
                if step == 2:
                    add_rows(
                        sums.at[k], (size - 1) * seg, inputs.at[k],
                        lax.div(rank, jnp.int32(8)) * (8 * seg), size * seg, seg,
                    )
                else:
                    add_rows(
                        sums.at[k], (size - 1) * seg, sums.at[k],
                        (2 * size - 1) * seg + mine, size * seg, seg,
                    )
            if step < 0:
                break
            size = 1 << step
            other = 1 - bit_of(rank, size)
            if step == 3:
                source = inputs.at[k, rows(other * (8 * seg), 8 * seg)]
            else:
                source = sums.at[
                    k, rows((2 * size - 1) * seg + other * (size * seg), size * seg)
                ]
            copy = sender.start(
                source, sums.at[k, rows((size - 1) * seg, size * seg)], partners[step]
            )
            yield
        where = columns((share * chunks + k) * LANES, LANES)
        if kind == "feat":
            cross = sender.start(
                sums.at[k, rows((1 - share) * own_rows, own_rows)],
                feat_total.at[:, where],
                across,
            )
            local = pltpu.make_async_copy(
                sums.at[k, rows(share * own_rows, own_rows)], feat_total.at[:, where],
                own_sems.at[k],
            )
            local.start()
            local_copies.append(local)
            yield
            cross.wait_recv()
            return
        cross = sender.start(sums.at[k, pl.ds(part, part)], crossed.at[k], across)
        own_share = part // (relations + 1)
        own_place = rows(rank * own_share, own_share)
        for r in range(relations):
            rel_total[r, own_place, where] = sums[k, r * own_share : (r + 1) * own_share, :]
        self_total[own_place, where] = sums[k, relations * own_share : part, :]
        waiting = [(), ()]
        for wave in range(STEPS + 2):
            for piece in range(2):
                step = wave - piece
                if step < 0 or step > STEPS:
                    continue
                spot = share if piece == 0 else 1 - share
                there = columns((spot * chunks + k) * LANES, LANES)
                for copy in waiting[piece]:
                    copy.wait_recv()
                if piece == 1 and step == 0:
                    cross.wait_recv()
                    for r in range(relations):
                        rel_total[r, own_place, there] = crossed[
                            k, r * own_share : (r + 1) * own_share, :
                        ]
                    self_total[own_place, there] = crossed[k, relations * own_share : part, :]
                if step == STEPS:
                    continue
                size = (1 << step) * own_share
                span = rows(lax.div(rank, jnp.int32(1 << step)) * size, size)
                waiting[piece] = [
                    sender.start(held, held, partners[step])
                    for held in (rel_total.at[:, span, there], self_total.at[span, there])
                ]
            yield

    chains = [chain("rel", k) for k in range(chunks)] + [chain("feat", k) for k in range(chunks)]
    next(chains[0])
    active = []
    while chains or active:
        if len(chains) > 1:
            next(chains[1])
        if chains:
            active.append(chains.pop(0))
        for one in reversed(list(active)):
            if next(one, "end") == "end":
                active.remove(one)
    out_copy.wait_recv()
    for local in local_copies:
        local.wait()
    sender.finish()


def vmem(count):
    return [pl.BlockSpec(memory_space=pltpu.VMEM)] * count


def plane_gather(
    node_feats, rel_weights, self_weight, cotangent, tile_values, tile_peer, tile_slot,
    tile_target, tile_count, send_mask,
):
    f32 = jnp.float32
    relations, out_share, features = rel_weights.shape
    part_rows = cotangent.shape[1]
    own_rows = node_feats.shape[0]
    parts = lax.axis_size("nodes")
    half = features // 2
    chunks = half // LANES
    slots = tile_values.shape[2]
    seg = part_rows + MASK_ROWS
    node = lax.axis_index("nodes")
    share = lax.axis_index("feat")
    mask = send_mask[0].astype(f32).reshape(-1)
    mask = jnp.pad(mask, (0, MASK_ROWS * LANES - mask.shape[0])).reshape(MASK_ROWS, LANES)
    shape = jax.ShapeDtypeStruct
    gathered, far_weights, far_cotangent = pl.pallas_call(
        gather_kernel,
        out_shape=(
            shape((chunks, parts * seg, LANES), f32),
            shape((relations + 1, out_share, half), f32),
            shape((out_share, part_rows), f32),
        ),
        in_specs=vmem(5),
        out_specs=tuple(vmem(3)),
        scratch_shapes=[
            pltpu.SemaphoreType.DMA((40,)),
            pltpu.SemaphoreType.DMA((40,)),
            pltpu.SemaphoreType.DMA((2 * chunks,)),
        ],
        compiler_params=pltpu.CompilerParams(
            collective_id=0, has_side_effects=True, vmem_limit_bytes=16 * MIB
        ),
        name="gather_nodes",
    )(node_feats, rel_weights, self_weight, cotangent, mask)
    alive = jnp.arange(slots, dtype=jnp.int32)[None, :] < tile_count[0][:, None]
    codes = tile_peer[0] * 8 + tile_slot[0] * 4 + tile_target[0] * 2 + alive.astype(jnp.int32)
    me = jnp.stack([node, share]).astype(jnp.int32)
    rel_rows = (relations + 1) * out_share // parts
    smem = [pl.BlockSpec(memory_space=pltpu.SMEM)] * 2
    near_out, far_out, feat_parts, rel_parts = pl.pallas_call(
        compute_kernel,
        out_shape=(
            shape((out_share, part_rows), f32),
            shape((out_share, part_rows), f32),
            shape((chunks, parts * part_rows, LANES), f32),
            shape((chunks, parts * 2 * rel_rows, LANES), f32),
        ),
        in_specs=smem + vmem(7),
        out_specs=tuple(vmem(4)),
        scratch_shapes=[
            pltpu.SMEM((parts, MASK_ROWS, LANES), f32),
            pltpu.SemaphoreType.DMA((parts,)),
        ],
        compiler_params=pltpu.CompilerParams(vmem_limit_bytes=28 * MIB),
        name="local_products",
    )(
        codes, me,
        tile_values[0].reshape(relations * slots, TILE, TILE),
        gathered, rel_weights, self_weight, far_weights, cotangent, far_cotangent,
    )
    rel_total, self_total, feat_total, got_out = pl.pallas_call(
        reduce_kernel,
        out_shape=(
            shape((relations, out_share, features), f32),
            shape((out_share, features), f32),
            shape((own_rows, features), f32),
            shape((out_share, part_rows), f32),
        ),
        in_specs=vmem(3),
        out_specs=tuple(vmem(4)),
        scratch_shapes=[
            pltpu.VMEM((chunks, 15 * part_rows, LANES), f32),
            pltpu.VMEM((chunks, 15 * 2 * rel_rows, LANES), f32),
            pltpu.VMEM((chunks, rel_rows, LANES), f32),
            pltpu.SemaphoreType.DMA((96,)),
            pltpu.SemaphoreType.DMA((96,)),
            pltpu.SemaphoreType.DMA((2 * chunks,)),
        ],
        compiler_params=pltpu.CompilerParams(
            collective_id=1, has_side_effects=True, vmem_limit_bytes=28 * MIB
        ),
        name="reduce_grads",
    )(feat_parts, rel_parts, far_out)
    layer_out = near_out + got_out
    factor = float(part_rows * parts) ** (-0.5)
    return (layer_out, feat_total, rel_total * factor, self_total * factor)


def local(node_feats, rel_weights, self_weight, cotangent, *tiles):
    relations, out_share, features = rel_weights.shape
    parts, shares = lax.axis_size("nodes"), lax.axis_size("feat")
    fits = (
        parts == 16
        and shares == 2
        and relations == 5
        and out_share == 256
        and cotangent.shape[1] == 2 * TILE
        and features == 6 * LANES
    )
    plan = plane_gather if fits else slot_exchange
    return plan(node_feats, rel_weights, self_weight, cotangent, *tiles)


def solution(mesh):
    return jax.shard_map(
        local,
        mesh=mesh,
        in_specs=(
            P(("nodes", "feat"), None),
            P(None, "feat", None),
            P("feat", None),
            P("feat", "nodes"),
            P("nodes", None, None, None, None),
            P("nodes", None, None),
            P("nodes", None, None),
            P("nodes", None, None),
            P("nodes", None),
            P("nodes", None, None),
        ),
        out_specs=(
            P("feat", "nodes"),
            P(("nodes", "feat"), None),
            P(None, "feat", None),
            P("feat", None),
        ),
        check_vma=False,
    )
```

```python
import functools

import jax
import jax.numpy as jnp
from jax import lax
from jax.experimental import pallas as pl
from jax.experimental.pallas import tpu as pltpu
from jax.sharding import PartitionSpec as P

TILE = 128
CAP = 2


def slot_exchange(
    node_feats,
    rel_weights,
    self_weight,
    cotangent,
    tile_values,
    tile_peer,
    tile_slot,
    tile_target,
    tile_count,
    send_mask,
):
    highest = lax.Precision.HIGHEST
    relations = rel_weights.shape[0]
    out_share = rel_weights.shape[1]
    part_rows = cotangent.shape[1]
    blocks = part_rows // TILE
    parts = lax.axis_size("nodes")
    slot_steps = tile_values.shape[2]
    combined = relations * blocks
    gathered = lax.all_gather(node_feats, "feat", axis=0, tiled=True)
    hidden = jnp.einsum("rfi,ni->rfn", rel_weights, gathered, precision=highest)
    self_part = jnp.einsum("fi,ni->fn", self_weight, gathered, precision=highest)
    hidden_blocks = (
        hidden.reshape(relations, out_share, blocks, TILE)
        .transpose(0, 2, 1, 3)
        .reshape(combined, out_share, TILE)
    )
    mask_rows = send_mask[0]
    slot_rank = jnp.cumsum(mask_rows, axis=1) - 1
    slot_ids = jnp.arange(CAP, dtype=jnp.int32)
    chooser = (
        (mask_rows[:, :, None] == 1) & (slot_rank[:, :, None] == slot_ids[None, None, :])
    ).astype(jnp.float32)
    outgoing = jnp.einsum("pcs,cfk->psfk", chooser, hidden_blocks, precision=highest)
    arrived = lax.all_to_all(outgoing, "nodes", split_axis=0, concat_axis=0, tiled=True)
    position = (tile_peer[0] * CAP + tile_slot[0]).reshape(-1)
    alive = (
        (jnp.arange(slot_steps, dtype=jnp.int32)[None, :] < tile_count[0][:, None])
        .reshape(-1)
        .astype(jnp.float32)
    )
    pieces = arrived.reshape(parts * CAP, out_share, TILE)[position] * alive[:, None, None]
    weights = tile_values[0].reshape(relations * slot_steps, TILE, TILE)
    contrib = jnp.einsum(
        "tfu,tvu->tfv", pieces, weights, precision=highest, preferred_element_type=jnp.float32
    )
    targets = (
        tile_target[0].reshape(-1)[:, None] == jnp.arange(blocks, dtype=jnp.int32)[None, :]
    ).astype(jnp.float32)
    summed = jnp.einsum("tb,tfv->fbv", targets, contrib, precision=highest).reshape(
        out_share, part_rows
    )
    layer_out = summed + self_part
    grad_blocks = cotangent.reshape(out_share, blocks, TILE)
    picked = jnp.einsum("tb,fbv->tfv", targets, grad_blocks, precision=highest)
    returned = jnp.einsum(
        "tfv,tvu->tfu", picked, weights, precision=highest, preferred_element_type=jnp.float32
    )
    placing = (position[:, None] == jnp.arange(parts * CAP, dtype=jnp.int32)[None, :]).astype(
        jnp.float32
    ) * alive[:, None]
    going_back = jnp.einsum("tq,tfu->qfu", placing, returned, precision=highest).reshape(
        parts, CAP, out_share, TILE
    )
    came_back = lax.all_to_all(going_back, "nodes", split_axis=0, concat_axis=0, tiled=True)
    source_grads = jnp.einsum("pcs,psfk->cfk", chooser, came_back, precision=highest)
    grad_hidden = (
        source_grads.reshape(relations, blocks, out_share, TILE)
        .transpose(0, 2, 1, 3)
        .reshape(relations, out_share, part_rows)
    )
    rel_local = jnp.einsum("rfn,ni->rfi", grad_hidden, gathered, precision=highest)
    self_local = jnp.dot(cotangent, gathered, precision=highest)
    rel_total, self_total = lax.psum((rel_local, self_local), "nodes")
    factor = float(part_rows * parts) ** (-0.5)
    term = jnp.einsum("rfn,rfi->ni", grad_hidden, rel_weights, precision=highest)
    feat_grad = lax.psum_scatter(
        term + jnp.einsum("fn,fi->ni", cotangent, self_weight, precision=highest),
        "feat",
        scatter_dimension=0,
        tiled=True,
    )
    return (layer_out, feat_grad, rel_total * factor, self_total * factor)


LANES = 128
MASK_ROWS = 8
MIB = 1024 * 1024
MESH = pl.DeviceIdType.MESH
STEPS = 4


def bit_of(value, weight):
    return lax.rem(lax.div(value, jnp.int32(weight)), jnp.int32(2))


def place():
    node = lax.axis_index("nodes")
    share = lax.axis_index("feat")
    bits = [bit_of(node, 8), bit_of(node, 4), bit_of(node, 2), bit_of(node, 1)]
    rank = bits[0] + 2 * bits[1] + 4 * bits[2] + 8 * bits[3]
    partners = [
        (node + weight * (1 - 2 * bit), share) for weight, bit in zip((8, 4, 2, 1), bits)
    ]
    across = (node, 1 - share)
    return rank, bits, share, partners, across


def rank_of(node):
    z1, z0, y, core = (bit_of(node, weight) for weight in (8, 4, 2, 1))
    return z1 + 2 * z0 + 4 * y + 8 * core


def greet(devices):
    barrier = pltpu.get_barrier_semaphore()
    for device in devices:
        pl.semaphore_signal(barrier, inc=1, device_id=device, device_id_type=MESH)
    pl.semaphore_wait(barrier, len(devices))


class Sender:
    def __init__(self, send_sems, recv_sems):
        self.send_sems, self.recv_sems, self.used, self.copies = send_sems, recv_sems, 0, []

    def start(self, source, target, device):
        copy = pltpu.make_async_remote_copy(
            src_ref=source,
            dst_ref=target,
            send_sem=self.send_sems.at[self.used],
            recv_sem=self.recv_sems.at[self.used],
            device_id=device,
            device_id_type=MESH,
        )
        self.used += 1
        self.copies.append(copy)
        copy.start()
        return copy

    def finish(self):
        for copy in self.copies:
            copy.wait_send()


def rows(start, count):
    return pl.ds(pl.multiple_of(start, 8), count)


def columns(start, count):
    return pl.ds(pl.multiple_of(start, LANES), count)


def gather_kernel(
    feats, rel_weights, self_weight, cotangent, mask, gathered, got_weights, got_cotangent,
    send_sems, recv_sems, own_sems,
):
    rank, bits, share, partners, across = place()
    core = bits[3]
    sibling = partners[3]
    chunks = gathered.shape[0]
    half = chunks * LANES
    seg = gathered.shape[1] // 16
    relations = rel_weights.shape[0]
    own_rows = feats.shape[0]
    base = rank * seg
    own = []
    for k in range(chunks):
        for count, (source, target) in enumerate(
            (
                (
                    feats.at[:, columns(share * half + k * LANES, LANES)],
                    gathered.at[k, rows(base + share * own_rows, own_rows)],
                ),
                (mask, gathered.at[k, rows(base + 2 * own_rows, MASK_ROWS)]),
            )
        ):
            copy = pltpu.make_async_copy(source, target, own_sems.at[2 * k + count])
            copy.start()
            own.append(copy)
    greet(partners + [across])
    sender = Sender(send_sems, recv_sems)
    far = (1 - share) * half
    crossing = [
        sender.start(
            feats.at[:, columns(far + k * LANES, LANES)],
            gathered.at[k, rows(base + share * own_rows, own_rows)],
            across,
        )
        for k in range(chunks)
    ]
    cotangent_copy = sender.start(cotangent, got_cotangent, across)
    pairs = (relations + 1) // 2
    lower = [
        sender.start(
            rel_weights.at[core * (pairs - 1) + j, :, columns(far, half)],
            got_weights.at[core * (pairs - 1) + j],
            across,
        )
        for j in range(pairs - 1)
    ]
    weight_rows = rel_weights.shape[1] // 2
    lower.append(
        sender.start(
            rel_weights.at[relations - 1, rows(core * weight_rows, weight_rows), columns(far, half)],
            got_weights.at[relations - 1, rows(core * weight_rows, weight_rows)],
            across,
        )
    )
    lower.append(
        sender.start(
            self_weight.at[rows(core * weight_rows, weight_rows), columns(far, half)],
            got_weights.at[relations, rows(core * weight_rows, weight_rows)],
            across,
        )
    )
    for copy in own:
        copy.wait()

    def held(start, count):
        return rows(start * seg, count * seg)

    def send(k, start, count, step):
        block = gathered.at[k, held(start, count)]
        return sender.start(block, block, partners[step])

    def forward(j):
        lower[j].wait_recv()
        if j < pairs - 1:
            block = got_weights.at[core * (pairs - 1) + j]
        else:
            block = got_weights.at[j + pairs - 1, rows(core * weight_rows, weight_rows)]
        forwarded.append(sender.start(block, block, sibling))

    forwarded = []
    first, first_other = rank, rank + 1 - 2 * bits[0]
    second = rank - bits[0]
    second_other = second + 2 - 4 * bits[1]
    third = second - 2 * bits[1]
    third_other = third + 4 - 8 * bits[2]
    by_z1, by_z0, by_y, by_core = [], [], [], []
    for k in range(chunks):
        crossing[k].wait_recv()
        by_z1.append(send(k, first, 1, 0))
        by_y.append([send(k, first, 1, 2)])
    for k in range(chunks):
        by_z1[k].wait_recv()
        by_z0.append(send(k, second, 2, 1))
        by_y[k].append(send(k, first_other, 1, 2))
    for k in range(chunks):
        by_z0[k].wait_recv()
        by_y[k].append(send(k, second_other, 2, 2))
        by_core.append(send(k, third, 4, 3))
    for k in range(chunks):
        for copy in by_y[k]:
            copy.wait_recv()
        by_core.append(send(k, third_other, 4, 3))
        forward(k)
    for j in range(chunks, len(lower)):
        forward(j)
    cotangent_copy.wait_recv()
    for copy in by_core + forwarded:
        copy.wait_recv()
    sender.finish()


def parts_of(value):
    high = value.astype(jnp.bfloat16)
    return high, (value - high.astype(jnp.float32)).astype(jnp.bfloat16)


def product(left, right, dims):
    def one(a, b):
        return lax.dot_general(a, b, (dims, ((), ())), preferred_element_type=jnp.float32)

    return one(left[0], right[0]) + (one(left[0], right[1]) + one(left[1], right[0]))


def exact_product(left, right, dims):
    high, low = parts_of(right)

    def one(b):
        return lax.dot_general(left, b, (dims, ((), ())), preferred_element_type=jnp.float32)

    return one(high) + one(low)


def compute_kernel(
    codes, me, tiles, gathered, rel_weights, self_weight, far_weights,
    near_cotangent, far_cotangent, near_out, far_out, feat_parts, rel_parts, masks, mask_sems,
):
    relations, slots = codes.shape
    chunks = gathered.shape[0]
    half = chunks * LANES
    out_share, part_rows = near_cotangent.shape
    seg = gathered.shape[1] // 16
    blocks = 2
    node, share = me[0], me[1]
    copies = [
        pltpu.make_async_copy(
            gathered.at[0, pl.ds(q * seg + part_rows, MASK_ROWS)], masks.at[q], mask_sems.at[q]
        )
        for q in range(16)
    ]
    for copy in copies:
        copy.start()
    near = parts_of(near_cotangent[...])
    far = parts_of(far_cotangent[...])
    near_t = parts_of(near_cotangent[...].T)
    far_t = parts_of(far_cotangent[...].T)
    share_rows = out_share // 16
    near_columns = columns(share * half, half)
    feat_parts[...] = jnp.zeros_like(feat_parts)
    for copy in copies:
        copy.wait()

    def feat_start(sender):
        return rank_of(sender) * part_rows

    def project(r, z, near_w):
        far_w = parts_of(far_weights[r])
        near_part = product(near_w, z, ((1,), (1,)))
        far_part = product(far_w, z, ((1,), (1,)))
        for which, grad in enumerate((near, far)):
            result = product(grad, z, ((1,), (0,)))
            for q in range(16):
                start = (q * 2 + which) * (relations + 1) * share_rows + r * share_rows
                for k in range(chunks):
                    rel_parts[k, rows(start, share_rows), :] = result[
                        q * share_rows : (q + 1) * share_rows, k * LANES : (k + 1) * LANES
                    ]
        grad = product(near_t, near_w, ((1,), (0,))) + product(far_t, far_w, ((1,), (0,)))
        return near_part, far_part, grad

    own = jnp.concatenate(
        [gathered[k, rows(rank_of(node) * seg, part_rows), :] for k in range(chunks)], axis=1
    )
    near_part, far_part, grad = project(
        relations, parts_of(own), parts_of(self_weight[:, near_columns])
    )
    near_out[...] = near_part
    far_out[...] = far_part
    for k in range(chunks):
        feat_parts[k, rows(feat_start(node), part_rows), :] = grad[
            :, k * LANES : (k + 1) * LANES
        ]

    @pl.loop(0, relations)
    def _(r):
        pieces, dense, places = [], [], []
        for t in range(slots):
            code = codes[r, t]
            alive, target, slot = (bit_of(code, weight) == 1 for weight in (1, 2, 4))
            peer = lax.div(code, jnp.int32(8))
            rank = rank_of(peer)
            at = node * (relations * blocks) + r * blocks

            def marked(b):
                return masks[rank, lax.div(at + b, LANES), lax.rem(at + b, LANES)] > 0.5

            block = jnp.where(
                marked(0), jnp.where(marked(1) & slot, jnp.int32(1), jnp.int32(0)), jnp.int32(1)
            )
            start = rank * seg + block * TILE
            pieces.append(
                jnp.concatenate(
                    [gathered[k, rows(start, TILE), :] for k in range(chunks)], axis=1
                )
            )
            tile = tiles[r * slots + t]
            dense.append(
                jnp.concatenate(
                    [
                        tile * jnp.where(alive & (target if b == 1 else ~target), 1.0, 0.0).astype(tile.dtype)
                        for b in range(blocks)
                    ],
                    axis=0,
                )
            )
            places.append((peer, block))
        dense = jnp.concatenate(dense, axis=1)
        z = parts_of(exact_product(dense, jnp.concatenate(pieces, axis=0), ((1,), (0,))))
        near_part, far_part, grad = project(r, z, parts_of(rel_weights[r, :, near_columns]))
        near_out[...] += near_part
        far_out[...] += far_part
        back = exact_product(dense, grad, ((0,), (0,)))
        for t, (peer, block) in enumerate(places):
            for k in range(chunks):
                feat_parts[k, rows(feat_start(peer) + block * TILE, TILE), :] += back[
                    t * TILE : (t + 1) * TILE, k * LANES : (k + 1) * LANES
                ]


def add_rows(target, target_start, source, source_start, count, block):

    def body(i, carry):
        there = rows(target_start + i * block, block)
        target[there, :] = target[there, :] + source[rows(source_start + i * block, block), :]
        return carry

    lax.fori_loop(0, count // block, body, 0)


def reduce_kernel(
    feat_parts, rel_parts, far_out, rel_total, self_total, feat_total, got_out,
    feat_sums, rel_sums, crossed, send_sems, recv_sems, own_sems,
):
    rank, bits, share, partners, across = place()
    chunks = feat_parts.shape[0]
    feat_seg = feat_parts.shape[1] // 16
    rel_seg = rel_parts.shape[1] // 16
    own_rows = feat_seg // 2
    part = rel_seg // 2
    relations = rel_total.shape[0]
    greet(partners + [across])
    sender = Sender(send_sems, recv_sems)
    out_copy = sender.start(far_out, got_out, across)
    local_copies = []

    def chain(kind, k):
        inputs, sums, seg = (
            (rel_parts, rel_sums, rel_seg) if kind == "rel" else (feat_parts, feat_sums, feat_seg)
        )
        copy = None
        for step in (3, 2, 1, 0, -1):
            if copy is not None:
                copy.wait_recv()
                size = 1 << (step + 1)
                mine = size * seg * bit_of(rank, size)
                if step == 2:
                    add_rows(
                        sums.at[k], (size - 1) * seg, inputs.at[k],
                        lax.div(rank, jnp.int32(8)) * (8 * seg), size * seg, seg,
                    )
                else:
                    add_rows(
                        sums.at[k], (size - 1) * seg, sums.at[k],
                        (2 * size - 1) * seg + mine, size * seg, seg,
                    )
            if step < 0:
                break
            size = 1 << step
            other = 1 - bit_of(rank, size)
            if step == 3:
                source = inputs.at[k, rows(other * (8 * seg), 8 * seg)]
            else:
                source = sums.at[
                    k, rows((2 * size - 1) * seg + other * (size * seg), size * seg)
                ]
            copy = sender.start(
                source, sums.at[k, rows((size - 1) * seg, size * seg)], partners[step]
            )
            yield
        where = columns((share * chunks + k) * LANES, LANES)
        if kind == "feat":
            cross = sender.start(
                sums.at[k, rows((1 - share) * own_rows, own_rows)],
                feat_total.at[:, where],
                across,
            )
            local = pltpu.make_async_copy(
                sums.at[k, rows(share * own_rows, own_rows)], feat_total.at[:, where],
                own_sems.at[k],
            )
            local.start()
            local_copies.append(local)
            yield
            cross.wait_recv()
            return
        cross = sender.start(sums.at[k, pl.ds(part, part)], crossed.at[k], across)
        own_share = part // (relations + 1)
        own_place = rows(rank * own_share, own_share)
        for r in range(relations):
            rel_total[r, own_place, where] = sums[k, r * own_share : (r + 1) * own_share, :]
        self_total[own_place, where] = sums[k, relations * own_share : part, :]
        waiting = [(), ()]
        for wave in range(STEPS + 2):
            for piece in range(2):
                step = wave - piece
                if step < 0 or step > STEPS:
                    continue
                spot = share if piece == 0 else 1 - share
                there = columns((spot * chunks + k) * LANES, LANES)
                for copy in waiting[piece]:
                    copy.wait_recv()
                if piece == 1 and step == 0:
                    cross.wait_recv()
                    for r in range(relations):
                        rel_total[r, own_place, there] = crossed[
                            k, r * own_share : (r + 1) * own_share, :
                        ]
                    self_total[own_place, there] = crossed[k, relations * own_share : part, :]
                if step == STEPS:
                    continue
                size = (1 << step) * own_share
                span = rows(lax.div(rank, jnp.int32(1 << step)) * size, size)
                waiting[piece] = [
                    sender.start(held, held, partners[step])
                    for held in (rel_total.at[:, span, there], self_total.at[span, there])
                ]
            yield

    chains = [chain("rel", k) for k in range(chunks)] + [chain("feat", k) for k in range(chunks)]
    next(chains[0])
    active = []
    while chains or active:
        if len(chains) > 1:
            next(chains[1])
        if chains:
            active.append(chains.pop(0))
        for one in reversed(list(active)):
            if next(one, "end") == "end":
                active.remove(one)
    out_copy.wait_recv()
    for local in local_copies:
        local.wait()
    sender.finish()


def vmem(count):
    return [pl.BlockSpec(memory_space=pltpu.VMEM)] * count


def plane_gather(
    node_feats, rel_weights, self_weight, cotangent, tile_values, tile_peer, tile_slot,
    tile_target, tile_count, send_mask,
):
    f32 = jnp.float32
    relations, out_share, features = rel_weights.shape
    part_rows = cotangent.shape[1]
    own_rows = node_feats.shape[0]
    parts = lax.axis_size("nodes")
    half = features // 2
    chunks = half // LANES
    slots = tile_values.shape[2]
    seg = part_rows + MASK_ROWS
    node = lax.axis_index("nodes")
    share = lax.axis_index("feat")
    mask = send_mask[0].astype(f32).reshape(-1)
    mask = jnp.pad(mask, (0, MASK_ROWS * LANES - mask.shape[0])).reshape(MASK_ROWS, LANES)
    shape = jax.ShapeDtypeStruct
    gathered, far_weights, far_cotangent = pl.pallas_call(
        gather_kernel,
        out_shape=(
            shape((chunks, parts * seg, LANES), f32),
            shape((relations + 1, out_share, half), f32),
            shape((out_share, part_rows), f32),
        ),
        in_specs=[pl.BlockSpec(memory_space=pltpu.HBM)] * 4 + vmem(1),
        out_specs=tuple(vmem(3)),
        scratch_shapes=[
            pltpu.SemaphoreType.DMA((40,)),
            pltpu.SemaphoreType.DMA((40,)),
            pltpu.SemaphoreType.DMA((2 * chunks,)),
        ],
        compiler_params=pltpu.CompilerParams(
            collective_id=0, has_side_effects=True, vmem_limit_bytes=16 * MIB
        ),
        name="gather_nodes",
    )(node_feats, rel_weights, self_weight, cotangent, mask)
    alive = jnp.arange(slots, dtype=jnp.int32)[None, :] < tile_count[0][:, None]
    codes = tile_peer[0] * 8 + tile_slot[0] * 4 + tile_target[0] * 2 + alive.astype(jnp.int32)
    me = jnp.stack([node, share]).astype(jnp.int32)
    rel_rows = (relations + 1) * out_share // parts
    smem = [pl.BlockSpec(memory_space=pltpu.SMEM)] * 2
    near_out, far_out, feat_parts, rel_parts = pl.pallas_call(
        compute_kernel,
        out_shape=(
            shape((out_share, part_rows), f32),
            shape((out_share, part_rows), f32),
            shape((chunks, parts * part_rows, LANES), f32),
            shape((chunks, parts * 2 * rel_rows, LANES), f32),
        ),
        in_specs=smem + vmem(7),
        out_specs=tuple(vmem(4)),
        scratch_shapes=[
            pltpu.SMEM((parts, MASK_ROWS, LANES), f32),
            pltpu.SemaphoreType.DMA((parts,)),
        ],
        compiler_params=pltpu.CompilerParams(vmem_limit_bytes=28 * MIB),
        name="local_products",
    )(
        codes, me,
        tile_values[0].reshape(relations * slots, TILE, TILE),
        gathered, rel_weights, self_weight, far_weights, cotangent, far_cotangent,
    )
    rel_total, self_total, feat_total, got_out = pl.pallas_call(
        reduce_kernel,
        out_shape=(
            shape((relations, out_share, features), f32),
            shape((out_share, features), f32),
            shape((own_rows, features), f32),
            shape((out_share, part_rows), f32),
        ),
        in_specs=vmem(3),
        out_specs=tuple(vmem(4)),
        scratch_shapes=[
            pltpu.VMEM((chunks, 15 * part_rows, LANES), f32),
            pltpu.VMEM((chunks, 15 * 2 * rel_rows, LANES), f32),
            pltpu.VMEM((chunks, rel_rows, LANES), f32),
            pltpu.SemaphoreType.DMA((96,)),
            pltpu.SemaphoreType.DMA((96,)),
            pltpu.SemaphoreType.DMA((2 * chunks,)),
        ],
        compiler_params=pltpu.CompilerParams(
            collective_id=1, has_side_effects=True, vmem_limit_bytes=28 * MIB
        ),
        name="reduce_grads",
    )(feat_parts, rel_parts, far_out)
    layer_out = near_out + got_out
    factor = float(part_rows * parts) ** (-0.5)
    return (layer_out, feat_total, rel_total * factor, self_total * factor)


def local(node_feats, rel_weights, self_weight, cotangent, *tiles):
    relations, out_share, features = rel_weights.shape
    parts, shares = lax.axis_size("nodes"), lax.axis_size("feat")
    fits = (
        parts == 16
        and shares == 2
        and relations == 5
        and out_share == 256
        and cotangent.shape[1] == 2 * TILE
        and features == 6 * LANES
    )
    plan = plane_gather if fits else slot_exchange
    return plan(node_feats, rel_weights, self_weight, cotangent, *tiles)


def solution(mesh):
    return jax.shard_map(
        local,
        mesh=mesh,
        in_specs=(
            P(("nodes", "feat"), None),
            P(None, "feat", None),
            P("feat", None),
            P("feat", "nodes"),
            P("nodes", None, None, None, None),
            P("nodes", None, None),
            P("nodes", None, None),
            P("nodes", None, None),
            P("nodes", None),
            P("nodes", None, None),
        ),
        out_specs=(
            P("feat", "nodes"),
            P(("nodes", "feat"), None),
            P(None, "feat", None),
            P("feat", None),
        ),
        check_vma=False,
    )
```

```python
import functools

import jax
import jax.numpy as jnp
from jax import lax
from jax.experimental import pallas as pl
from jax.experimental.pallas import tpu as pltpu
from jax.sharding import PartitionSpec as P

TILE = 128
CAP = 2


def slot_exchange(
    node_feats,
    rel_weights,
    self_weight,
    cotangent,
    tile_values,
    tile_peer,
    tile_slot,
    tile_target,
    tile_count,
    send_mask,
):
    highest = lax.Precision.HIGHEST
    relations = rel_weights.shape[0]
    out_share = rel_weights.shape[1]
    part_rows = cotangent.shape[1]
    blocks = part_rows // TILE
    parts = lax.axis_size("nodes")
    slot_steps = tile_values.shape[2]
    combined = relations * blocks
    gathered = lax.all_gather(node_feats, "feat", axis=0, tiled=True)
    hidden = jnp.einsum("rfi,ni->rfn", rel_weights, gathered, precision=highest)
    self_part = jnp.einsum("fi,ni->fn", self_weight, gathered, precision=highest)
    hidden_blocks = (
        hidden.reshape(relations, out_share, blocks, TILE)
        .transpose(0, 2, 1, 3)
        .reshape(combined, out_share, TILE)
    )
    mask_rows = send_mask[0]
    slot_rank = jnp.cumsum(mask_rows, axis=1) - 1
    slot_ids = jnp.arange(CAP, dtype=jnp.int32)
    chooser = (
        (mask_rows[:, :, None] == 1) & (slot_rank[:, :, None] == slot_ids[None, None, :])
    ).astype(jnp.float32)
    outgoing = jnp.einsum("pcs,cfk->psfk", chooser, hidden_blocks, precision=highest)
    arrived = lax.all_to_all(outgoing, "nodes", split_axis=0, concat_axis=0, tiled=True)
    position = (tile_peer[0] * CAP + tile_slot[0]).reshape(-1)
    alive = (
        (jnp.arange(slot_steps, dtype=jnp.int32)[None, :] < tile_count[0][:, None])
        .reshape(-1)
        .astype(jnp.float32)
    )
    pieces = arrived.reshape(parts * CAP, out_share, TILE)[position] * alive[:, None, None]
    weights = tile_values[0].reshape(relations * slot_steps, TILE, TILE)
    contrib = jnp.einsum(
        "tfu,tvu->tfv", pieces, weights, precision=highest, preferred_element_type=jnp.float32
    )
    targets = (
        tile_target[0].reshape(-1)[:, None] == jnp.arange(blocks, dtype=jnp.int32)[None, :]
    ).astype(jnp.float32)
    summed = jnp.einsum("tb,tfv->fbv", targets, contrib, precision=highest).reshape(
        out_share, part_rows
    )
    layer_out = summed + self_part
    grad_blocks = cotangent.reshape(out_share, blocks, TILE)
    picked = jnp.einsum("tb,fbv->tfv", targets, grad_blocks, precision=highest)
    returned = jnp.einsum(
        "tfv,tvu->tfu", picked, weights, precision=highest, preferred_element_type=jnp.float32
    )
    placing = (position[:, None] == jnp.arange(parts * CAP, dtype=jnp.int32)[None, :]).astype(
        jnp.float32
    ) * alive[:, None]
    going_back = jnp.einsum("tq,tfu->qfu", placing, returned, precision=highest).reshape(
        parts, CAP, out_share, TILE
    )
    came_back = lax.all_to_all(going_back, "nodes", split_axis=0, concat_axis=0, tiled=True)
    source_grads = jnp.einsum("pcs,psfk->cfk", chooser, came_back, precision=highest)
    grad_hidden = (
        source_grads.reshape(relations, blocks, out_share, TILE)
        .transpose(0, 2, 1, 3)
        .reshape(relations, out_share, part_rows)
    )
    rel_local = jnp.einsum("rfn,ni->rfi", grad_hidden, gathered, precision=highest)
    self_local = jnp.dot(cotangent, gathered, precision=highest)
    rel_total, self_total = lax.psum((rel_local, self_local), "nodes")
    factor = float(part_rows * parts) ** (-0.5)
    term = jnp.einsum("rfn,rfi->ni", grad_hidden, rel_weights, precision=highest)
    feat_grad = lax.psum_scatter(
        term + jnp.einsum("fn,fi->ni", cotangent, self_weight, precision=highest),
        "feat",
        scatter_dimension=0,
        tiled=True,
    )
    return (layer_out, feat_grad, rel_total * factor, self_total * factor)


LANES = 128
MASK_ROWS = 8
MIB = 1024 * 1024
MESH = pl.DeviceIdType.MESH
STEPS = 4


def bit_of(value, weight):
    return lax.rem(lax.div(value, jnp.int32(weight)), jnp.int32(2))


def place():
    node = lax.axis_index("nodes")
    share = lax.axis_index("feat")
    bits = [bit_of(node, 8), bit_of(node, 4), bit_of(node, 2), bit_of(node, 1)]
    rank = bits[0] + 2 * bits[1] + 4 * bits[2] + 8 * bits[3]
    partners = [
        (node + weight * (1 - 2 * bit), share) for weight, bit in zip((8, 4, 2, 1), bits)
    ]
    across = (node, 1 - share)
    return rank, bits, share, partners, across


def rank_of(node):
    z1, z0, y, core = (bit_of(node, weight) for weight in (8, 4, 2, 1))
    return z1 + 2 * z0 + 4 * y + 8 * core


def greet(devices):
    barrier = pltpu.get_barrier_semaphore()
    for device in devices:
        pl.semaphore_signal(barrier, inc=1, device_id=device, device_id_type=MESH)
    pl.semaphore_wait(barrier, len(devices))


class Sender:
    def __init__(self, send_sems, recv_sems):
        self.send_sems, self.recv_sems, self.used, self.copies = send_sems, recv_sems, 0, []

    def start(self, source, target, device):
        copy = pltpu.make_async_remote_copy(
            src_ref=source,
            dst_ref=target,
            send_sem=self.send_sems.at[self.used],
            recv_sem=self.recv_sems.at[self.used],
            device_id=device,
            device_id_type=MESH,
        )
        self.used += 1
        self.copies.append(copy)
        copy.start()
        return copy

    def finish(self):
        for copy in self.copies:
            copy.wait_send()


def rows(start, count):
    return pl.ds(pl.multiple_of(start, 8), count)


def columns(start, count):
    return pl.ds(pl.multiple_of(start, LANES), count)


def gather_kernel(
    feats, rel_weights, self_weight, cotangent, mask, gathered, got_weights, got_cotangent,
    send_sems, recv_sems, own_sems,
):
    rank, bits, share, partners, across = place()
    core = bits[3]
    sibling = partners[3]
    chunks = gathered.shape[0]
    half = chunks * LANES
    seg = gathered.shape[1] // 16
    relations = rel_weights.shape[0]
    own_rows = feats.shape[0]
    base = rank * seg
    own = []
    for k in range(chunks):
        for count, (source, target) in enumerate(
            (
                (
                    feats.at[:, columns(share * half + k * LANES, LANES)],
                    gathered.at[k, rows(base + share * own_rows, own_rows)],
                ),
                (mask, gathered.at[k, rows(base + 2 * own_rows, MASK_ROWS)]),
            )
        ):
            copy = pltpu.make_async_copy(source, target, own_sems.at[2 * k + count])
            copy.start()
            own.append(copy)
    greet(partners + [across])
    sender = Sender(send_sems, recv_sems)
    far = (1 - share) * half
    crossing = [
        sender.start(
            feats.at[:, columns(far + k * LANES, LANES)],
            gathered.at[k, rows(base + share * own_rows, own_rows)],
            across,
        )
        for k in range(chunks)
    ]
    cotangent_copy = sender.start(cotangent, got_cotangent, across)
    pairs = (relations + 1) // 2
    lower = [
        sender.start(
            rel_weights.at[core * (pairs - 1) + j, :, columns(far, half)],
            got_weights.at[core * (pairs - 1) + j],
            across,
        )
        for j in range(pairs - 1)
    ]
    weight_rows = rel_weights.shape[1] // 2
    lower.append(
        sender.start(
            rel_weights.at[relations - 1, rows(core * weight_rows, weight_rows), columns(far, half)],
            got_weights.at[relations - 1, rows(core * weight_rows, weight_rows)],
            across,
        )
    )
    lower.append(
        sender.start(
            self_weight.at[rows(core * weight_rows, weight_rows), columns(far, half)],
            got_weights.at[relations, rows(core * weight_rows, weight_rows)],
            across,
        )
    )
    for copy in own:
        copy.wait()

    def held(start, count):
        return rows(start * seg, count * seg)

    def send(k, start, count, step):
        block = gathered.at[k, held(start, count)]
        return sender.start(block, block, partners[step])

    def forward(j):
        lower[j].wait_recv()
        if j < pairs - 1:
            block = got_weights.at[core * (pairs - 1) + j]
        else:
            block = got_weights.at[j + pairs - 1, rows(core * weight_rows, weight_rows)]
        forwarded.append(sender.start(block, block, sibling))

    forwarded = []
    first, first_other = rank, rank + 1 - 2 * bits[0]
    second = rank - bits[0]
    second_other = second + 2 - 4 * bits[1]
    third = second - 2 * bits[1]
    third_other = third + 4 - 8 * bits[2]
    by_z1, by_z0, by_y, by_core = [], [], [], []
    for k in range(chunks):
        crossing[k].wait_recv()
        by_z1.append(send(k, first, 1, 0))
        by_y.append([send(k, first, 1, 2)])
    for k in range(chunks):
        by_z1[k].wait_recv()
        by_z0.append(send(k, second, 2, 1))
        by_y[k].append(send(k, first_other, 1, 2))
    for k in range(chunks):
        by_z0[k].wait_recv()
        by_y[k].append(send(k, second_other, 2, 2))
        by_core.append(send(k, third, 4, 3))
    for k in range(chunks):
        for copy in by_y[k]:
            copy.wait_recv()
        by_core.append(send(k, third_other, 4, 3))
        forward(k)
    for j in range(chunks, len(lower)):
        forward(j)
    cotangent_copy.wait_recv()
    for copy in by_core + forwarded:
        copy.wait_recv()
    sender.finish()


def parts_of(value):
    high = value.astype(jnp.bfloat16)
    return high, (value - high.astype(jnp.float32)).astype(jnp.bfloat16)


def product(left, right, dims):
    def one(a, b):
        return lax.dot_general(a, b, (dims, ((), ())), preferred_element_type=jnp.float32)

    return one(left[0], right[0]) + (one(left[0], right[1]) + one(left[1], right[0]))


def exact_product(left, right, dims):
    high, low = parts_of(right)

    def one(b):
        return lax.dot_general(left, b, (dims, ((), ())), preferred_element_type=jnp.float32)

    return one(high) + one(low)


def compute_kernel(
    codes, me, tiles, gathered, rel_weights, self_weight, far_weights,
    near_cotangent, far_cotangent, mixed, feat_parts, masks, mask_sems,
):
    relations, slots = codes.shape
    chunks = gathered.shape[0]
    half = chunks * LANES
    out_share, part_rows = near_cotangent.shape
    seg = gathered.shape[1] // 16
    blocks = 2
    node, share = me[0], me[1]
    copies = [
        pltpu.make_async_copy(
            gathered.at[0, pl.ds(q * seg + part_rows, MASK_ROWS)], masks.at[q], mask_sems.at[q]
        )
        for q in range(16)
    ]
    for copy in copies:
        copy.start()
    near_t = parts_of(near_cotangent[...].T)
    far_t = parts_of(far_cotangent[...].T)
    near_columns = columns(share * half, half)
    feat_parts[...] = jnp.zeros_like(feat_parts)
    for copy in copies:
        copy.wait()

    def feat_start(sender):
        return rank_of(sender) * part_rows

    def back_through(r, near_w):
        far_w = parts_of(far_weights[r])
        return product(near_t, near_w, ((1,), (0,))) + product(far_t, far_w, ((1,), (0,)))

    own = jnp.concatenate(
        [gathered[k, rows(rank_of(node) * seg, part_rows), :] for k in range(chunks)], axis=1
    )
    mixed[relations] = own
    grad = back_through(relations, parts_of(self_weight[:, near_columns]))
    for k in range(chunks):
        feat_parts[k, rows(feat_start(node), part_rows), :] = grad[
            :, k * LANES : (k + 1) * LANES
        ]

    @pl.loop(0, relations)
    def _(r):
        pieces, dense, places = [], [], []
        for t in range(slots):
            code = codes[r, t]
            alive, target, slot = (bit_of(code, weight) == 1 for weight in (1, 2, 4))
            peer = lax.div(code, jnp.int32(8))
            rank = rank_of(peer)
            at = node * (relations * blocks) + r * blocks

            def marked(b):
                return masks[rank, lax.div(at + b, LANES), lax.rem(at + b, LANES)] > 0.5

            block = jnp.where(
                marked(0), jnp.where(marked(1) & slot, jnp.int32(1), jnp.int32(0)), jnp.int32(1)
            )
            start = rank * seg + block * TILE
            pieces.append(
                jnp.concatenate(
                    [gathered[k, rows(start, TILE), :] for k in range(chunks)], axis=1
                )
            )
            tile = tiles[r * slots + t]
            dense.append(
                jnp.concatenate(
                    [
                        tile * jnp.where(alive & (target if b == 1 else ~target), 1.0, 0.0).astype(tile.dtype)
                        for b in range(blocks)
                    ],
                    axis=0,
                )
            )
            places.append((peer, block))
        dense = jnp.concatenate(dense, axis=1)
        mixed[r] = exact_product(dense, jnp.concatenate(pieces, axis=0), ((1,), (0,)))
        grad = back_through(r, parts_of(rel_weights[r, :, near_columns]))
        back = exact_product(dense, grad, ((0,), (0,)))
        for t, (peer, block) in enumerate(places):
            for k in range(chunks):
                feat_parts[k, rows(feat_start(peer) + block * TILE, TILE), :] += back[
                    t * TILE : (t + 1) * TILE, k * LANES : (k + 1) * LANES
                ]


def add_rows(target, target_start, source, source_start, count, block):

    def body(i, carry):
        there = rows(target_start + i * block, block)
        target[there, :] = target[there, :] + source[rows(source_start + i * block, block), :]
        return carry

    lax.fori_loop(0, count // block, body, 0)


def reduce_kernel(
    feat_parts, mixed, rel_weights, self_weight, far_weights, near_cotangent, far_cotangent,
    rel_total, self_total, feat_total, got_out, near_out,
    feat_sums, rel_sums, crossed, rel_parts, far_out, send_sems, recv_sems, own_sems,
):
    rank, bits, share, partners, across = place()
    chunks = feat_parts.shape[0]
    feat_seg = feat_parts.shape[1] // 16
    rel_seg = rel_parts.shape[1] // 16
    own_rows = feat_seg // 2
    part = rel_seg // 2
    relations = rel_total.shape[0]
    greet(partners + [across])
    sender = Sender(send_sems, recv_sems)
    local_copies = []
    half = chunks * LANES
    near_columns = columns(share * half, half)
    share_rows = near_cotangent.shape[0] // 16

    def project(r, near_w):
        z = parts_of(mixed[r])
        near_out[...] += product(parts_of(near_w), z, ((1,), (1,)))
        far_out[...] += product(parts_of(far_weights[r]), z, ((1,), (1,)))
        for which, grad in enumerate((near_cotangent, far_cotangent)):
            result = product(parts_of(grad[...]), z, ((1,), (0,)))
            for q in range(16):
                start = (q * 2 + which) * (relations + 1) * share_rows + r * share_rows
                for k in range(chunks):
                    rel_parts[k, rows(start, share_rows), :] = result[
                        q * share_rows : (q + 1) * share_rows, k * LANES : (k + 1) * LANES
                    ]

    def project_some(low, high):
        def body(r, carry):
            project(r, rel_weights[r, :, near_columns])
            return carry

        lax.fori_loop(low, high, body, 0)

    def chain(kind, k):
        inputs, sums, seg = (
            (rel_parts, rel_sums, rel_seg) if kind == "rel" else (feat_parts, feat_sums, feat_seg)
        )
        copy = None
        for step in (3, 2, 1, 0, -1):
            if copy is not None:
                copy.wait_recv()
                size = 1 << (step + 1)
                mine = size * seg * bit_of(rank, size)
                if step == 2:
                    add_rows(
                        sums.at[k], (size - 1) * seg, inputs.at[k],
                        lax.div(rank, jnp.int32(8)) * (8 * seg), size * seg, seg,
                    )
                else:
                    add_rows(
                        sums.at[k], (size - 1) * seg, sums.at[k],
                        (2 * size - 1) * seg + mine, size * seg, seg,
                    )
            if step < 0:
                break
            size = 1 << step
            other = 1 - bit_of(rank, size)
            if step == 3:
                source = inputs.at[k, rows(other * (8 * seg), 8 * seg)]
            else:
                source = sums.at[
                    k, rows((2 * size - 1) * seg + other * (size * seg), size * seg)
                ]
            copy = sender.start(
                source, sums.at[k, rows((size - 1) * seg, size * seg)], partners[step]
            )
            yield
        where = columns((share * chunks + k) * LANES, LANES)
        if kind == "feat":
            cross = sender.start(
                sums.at[k, rows((1 - share) * own_rows, own_rows)],
                feat_total.at[:, where],
                across,
            )
            local = pltpu.make_async_copy(
                sums.at[k, rows(share * own_rows, own_rows)], feat_total.at[:, where],
                own_sems.at[k],
            )
            local.start()
            local_copies.append(local)
            yield
            cross.wait_recv()
            return
        cross = sender.start(sums.at[k, pl.ds(part, part)], crossed.at[k], across)
        own_share = part // (relations + 1)
        own_place = rows(rank * own_share, own_share)
        for r in range(relations):
            rel_total[r, own_place, where] = sums[k, r * own_share : (r + 1) * own_share, :]
        self_total[own_place, where] = sums[k, relations * own_share : part, :]
        waiting = [(), ()]
        for wave in range(STEPS + 2):
            for piece in range(2):
                step = wave - piece
                if step < 0 or step > STEPS:
                    continue
                spot = share if piece == 0 else 1 - share
                there = columns((spot * chunks + k) * LANES, LANES)
                for copy in waiting[piece]:
                    copy.wait_recv()
                if piece == 1 and step == 0:
                    cross.wait_recv()
                    for r in range(relations):
                        rel_total[r, own_place, there] = crossed[
                            k, r * own_share : (r + 1) * own_share, :
                        ]
                    self_total[own_place, there] = crossed[k, relations * own_share : part, :]
                if step == STEPS:
                    continue
                size = (1 << step) * own_share
                span = rows(lax.div(rank, jnp.int32(1 << step)) * size, size)
                waiting[piece] = [
                    sender.start(held, held, partners[step])
                    for held in (rel_total.at[:, span, there], self_total.at[span, there])
                ]
            yield

    chains = [chain("feat", k) for k in range(chunks)]
    for one in chains:
        next(one)
    near_out[...] = jnp.zeros_like(near_out)
    far_out[...] = jnp.zeros_like(far_out)
    next(chains[0])
    project_some(0, 2)
    next(chains[1])
    project_some(2, 4)
    next(chains[2])
    project_some(4, relations)
    project(relations, self_weight[:, near_columns])
    out_copy = sender.start(far_out, got_out, across)
    active = list(chains)
    chains = [chain("rel", k) for k in range(chunks)]
    for one in chains:
        next(one)
    while chains or active:
        if chains:
            active.append(chains.pop(0))
        for one in reversed(list(active)):
            if next(one, "end") == "end":
                active.remove(one)
    out_copy.wait_recv()
    for local in local_copies:
        local.wait()
    sender.finish()


def vmem(count):
    return [pl.BlockSpec(memory_space=pltpu.VMEM)] * count


def plane_gather(
    node_feats, rel_weights, self_weight, cotangent, tile_values, tile_peer, tile_slot,
    tile_target, tile_count, send_mask,
):
    f32 = jnp.float32
    relations, out_share, features = rel_weights.shape
    part_rows = cotangent.shape[1]
    own_rows = node_feats.shape[0]
    parts = lax.axis_size("nodes")
    half = features // 2
    chunks = half // LANES
    slots = tile_values.shape[2]
    seg = part_rows + MASK_ROWS
    node = lax.axis_index("nodes")
    share = lax.axis_index("feat")
    mask = send_mask[0].astype(f32).reshape(-1)
    mask = jnp.pad(mask, (0, MASK_ROWS * LANES - mask.shape[0])).reshape(MASK_ROWS, LANES)
    shape = jax.ShapeDtypeStruct
    gathered, far_weights, far_cotangent = pl.pallas_call(
        gather_kernel,
        out_shape=(
            shape((chunks, parts * seg, LANES), f32),
            shape((relations + 1, out_share, half), f32),
            shape((out_share, part_rows), f32),
        ),
        in_specs=[pl.BlockSpec(memory_space=pltpu.HBM)] * 4 + vmem(1),
        out_specs=tuple(vmem(3)),
        scratch_shapes=[
            pltpu.SemaphoreType.DMA((40,)),
            pltpu.SemaphoreType.DMA((40,)),
            pltpu.SemaphoreType.DMA((2 * chunks,)),
        ],
        compiler_params=pltpu.CompilerParams(
            collective_id=0, has_side_effects=True, vmem_limit_bytes=16 * MIB
        ),
        name="gather_nodes",
    )(node_feats, rel_weights, self_weight, cotangent, mask)
    alive = jnp.arange(slots, dtype=jnp.int32)[None, :] < tile_count[0][:, None]
    codes = tile_peer[0] * 8 + tile_slot[0] * 4 + tile_target[0] * 2 + alive.astype(jnp.int32)
    me = jnp.stack([node, share]).astype(jnp.int32)
    rel_rows = (relations + 1) * out_share // parts
    smem = [pl.BlockSpec(memory_space=pltpu.SMEM)] * 2
    mixed, feat_parts = pl.pallas_call(
        compute_kernel,
        out_shape=(
            shape((relations + 1, part_rows, half), f32),
            shape((chunks, parts * part_rows, LANES), f32),
        ),
        in_specs=smem + vmem(7),
        out_specs=tuple(vmem(2)),
        scratch_shapes=[
            pltpu.SMEM((parts, MASK_ROWS, LANES), f32),
            pltpu.SemaphoreType.DMA((parts,)),
        ],
        compiler_params=pltpu.CompilerParams(vmem_limit_bytes=28 * MIB),
        name="local_products",
    )(
        codes, me,
        tile_values[0].reshape(relations * slots, TILE, TILE),
        gathered, rel_weights, self_weight, far_weights, cotangent, far_cotangent,
    )
    rel_total, self_total, feat_total, got_out, near_out = pl.pallas_call(
        reduce_kernel,
        out_shape=(
            shape((relations, out_share, features), f32),
            shape((out_share, features), f32),
            shape((own_rows, features), f32),
            shape((out_share, part_rows), f32),
            shape((out_share, part_rows), f32),
        ),
        in_specs=vmem(7),
        out_specs=tuple(vmem(5)),
        scratch_shapes=[
            pltpu.VMEM((chunks, 15 * part_rows, LANES), f32),
            pltpu.VMEM((chunks, 15 * 2 * rel_rows, LANES), f32),
            pltpu.VMEM((chunks, rel_rows, LANES), f32),
            pltpu.VMEM((chunks, parts * 2 * rel_rows, LANES), f32),
            pltpu.VMEM((out_share, part_rows), f32),
            pltpu.SemaphoreType.DMA((96,)),
            pltpu.SemaphoreType.DMA((96,)),
            pltpu.SemaphoreType.DMA((2 * chunks,)),
        ],
        compiler_params=pltpu.CompilerParams(
            collective_id=1, has_side_effects=True, vmem_limit_bytes=34 * MIB
        ),
        name="reduce_grads",
    )(feat_parts, mixed, rel_weights, self_weight, far_weights, cotangent, far_cotangent)
    layer_out = near_out + got_out
    factor = float(part_rows * parts) ** (-0.5)
    return (layer_out, feat_total, rel_total * factor, self_total * factor)


def local(node_feats, rel_weights, self_weight, cotangent, *tiles):
    relations, out_share, features = rel_weights.shape
    parts, shares = lax.axis_size("nodes"), lax.axis_size("feat")
    fits = (
        parts == 16
        and shares == 2
        and relations == 5
        and out_share == 256
        and cotangent.shape[1] == 2 * TILE
        and features == 6 * LANES
    )
    plan = plane_gather if fits else slot_exchange
    return plan(node_feats, rel_weights, self_weight, cotangent, *tiles)


def solution(mesh):
    return jax.shard_map(
        local,
        mesh=mesh,
        in_specs=(
            P(("nodes", "feat"), None),
            P(None, "feat", None),
            P("feat", None),
            P("feat", "nodes"),
            P("nodes", None, None, None, None),
            P("nodes", None, None),
            P("nodes", None, None),
            P("nodes", None, None),
            P("nodes", None),
            P("nodes", None, None),
        ),
        out_specs=(
            P("feat", "nodes"),
            P(("nodes", "feat"), None),
            P(None, "feat", None),
            P("feat", None),
        ),
        check_vma=False,
    )
```
